256 devices in a mesh: wrap: 256 (over x, z, y, core).
Axes of the slice: x: 4, y: 4, z: 8, core: 2. Of those that a mesh axis runs over, the one named last changes fastest.
Arguments:
- perturbation: float32 [5, 8192, 4, 256], P(None, 'wrap'), may hold values from -6 to 6
- advect_xi: float32 [8192, 256], P('wrap'), may hold values from -1 to 1
- advect_eta: float32 [8192, 256], P('wrap'), may hold values from -0.5 to 0.5
- sponge: float32 [8192, 256], P('wrap'), may hold values from 0.05 to 0.5
- couple_xi: float32 [5, 5], replicated, may hold values from -3 to 3
- couple_eta: float32 [5, 5], replicated, may hold values from -3 to 3
- couple_span: float32 [5, 5], replicated, may hold values from -3 to 3
- wake_cut: int32 [2], replicated, may hold values from 0 to 4096, as said below
- blowing: int32 [8192], P('wrap'), may hold values 0 or 1
Outputs:
- evolved: float32 [5, 8192, 4, 256], P(None, 'wrap')
The draws below stay inside these ranges and needn't reach their ends.
Inputs may be any that keep to these rules, and one draw needn't show every extreme that they name: wake_cut[0] < wake_cut[1] = 4096.
All inputs are finite; a program needn't handle non-finite values. No bound on the sum of `blowing` on one device may be relied on, other than what follows from the above.
Results may differ from the reference program's by a relative error of at most 0.0003.
Values sent between devices are 32-bit elements; how exact they have to be, the bound alone decides.
No kernel may reach another device: no remote copies, remote signals or barrier semaphores. Data moves between devices by JAX's collectives and lax.ppermute only.
A program may use at most 64 MiB of HBM per device.

```python
import math
import jax
import jax.numpy as jnp
from jax import lax

NJ = 256
K = 4
STEPS = 2
NI = 8192


def draw_wake_cut(key, part):
    key = jax.random.fold_in(key, 11)
    cut_start = jax.random.randint(key, (), 0, NI // 8 + 1)
    cut_end = jnp.zeros((), jnp.int32) + NI // 2
    return jnp.stack([cut_start, cut_end]).astype(jnp.int32)


def touch_ends(entries, own_key, least, top_value):
    longest = entries.shape.index(max(entries.shape))
    spots = []
    for shift in (0, 1):
        where = [jax.random.randint(jax.random.fold_in(own_key, axis), (), 0, length) for axis, length in enumerate(entries.shape)]
        where[longest] = (where[longest] + shift) % entries.shape[longest]
        spots.append(tuple(where))
    return entries.at[spots[0]].set(least).at[spots[1]].set(top_value)


def block_scale(stream_key, dims, split, least, top_value):
    loudness, own = 1.0, jax.random.fold_in(stream_key, 6)
    for position, parts in split:
        steps = jnp.exp(jax.random.uniform(jax.random.fold_in(own, position), (parts,), jnp.float32, least / len(split), top_value / len(split)))
        loudness = loudness * jnp.repeat(steps, dims[position] // parts).reshape([-1 if axis == position else 1 for axis in range(len(dims))])
    return loudness


def noise(key, dims, spread, bound, split=(), held_as=jnp.bfloat16):
    values = jax.random.normal(key, dims, jnp.float32) * spread
    if len(split) > 0:
        values = block_scale(key, dims, split, -0.22, 0.18) * values
    return jnp.clip(values, min=-bound, max=bound).astype(held_as)


def setup_inputs(seed: int = 0) -> dict:
    arg_keys = jax.random.split(jax.random.key(seed), 10)
    return {
        "perturbation": noise(arg_keys[0], (5, NI, K, NJ), 1.0, 6.0, ((1, 256),), jnp.float32),
        "advect_xi": jnp.clip(jax.random.uniform(arg_keys[1], (NI, NJ), jnp.float32, -1.0, 1.0) * block_scale(arg_keys[1], (NI, NJ), ((0, 256),), -0.4, 0.0), -1.0, 1.0),
        "advect_eta": jnp.clip(jax.random.uniform(arg_keys[2], (NI, NJ), jnp.float32, -0.5, 0.5) * block_scale(arg_keys[2], (NI, NJ), ((0, 256),), -0.4, 0.0), -0.5, 0.5),
        "sponge": jnp.clip(jnp.exp(math.log(0.5) - 2.3025851 * jax.random.uniform(arg_keys[3], (NI, NJ), jnp.float32) ** block_scale(arg_keys[3], (NI, NJ), ((0, 256),), -0.2, 0.2)), 0.05, 0.5),
        "couple_xi": noise(arg_keys[4], (5, 5), 0.3, 3.0, (), jnp.float32),
        "couple_eta": noise(arg_keys[5], (5, 5), 0.3, 3.0, (), jnp.float32),
        "couple_span": noise(arg_keys[6], (5, 5), 0.3, 3.0, (), jnp.float32),
        "wake_cut": draw_wake_cut(jax.random.fold_in(arg_keys[9], 71), 0),
        "blowing": touch_ends((jax.random.randint(arg_keys[8], (NI,), 0, 2) < 1).astype(jnp.int32), jax.random.fold_in(arg_keys[8], 1), 0, 1),
    }


time_step = 0.2
blow_gain = 1.0


def central(padded, direction, length):
    def shifted(offset):
        return lax.slice_in_dim(padded, 3 + offset, 3 + offset + length, axis=direction)
    return (45.0 * (shifted(1) - shifted(-1)) - 9.0 * (shifted(2) - shifted(-2)) + (shifted(3) - shifted(-3))) / 60.0


def flip_sign():
    return jnp.array([1.0, 1.0, -1.0, 1.0, 1.0], jnp.float32)[:, None, None, None]


def in_range(values, wake_cut):
    return (values >= wake_cut[0]) & (values < wake_cut[1])


def wall_ghost(wall_strip, wall_pressure, blow_rows, cut_rows, mirror_strip):
    reflected = wall_strip[:, :, :, ::-1] * flip_sign()
    lifted = reflected[2] + 2.0 * blow_gain * blow_rows[:, None, None] * wall_pressure[:, :, None]
    reflected = jnp.concatenate([reflected[:2], lifted[None], reflected[3:]], axis=0)
    mirrored = mirror_strip[:, :, :, ::-1] * flip_sign()
    return jnp.where(cut_rows[None, :, None, None], mirrored, reflected)


def couple(matrix, values):
    return jnp.einsum("cd,dikj->cikj", matrix, values, precision=lax.Precision.HIGHEST)


def linear_rhs(values, ghost_rows, padded_rows, advect_xi, advect_eta, sponge, couple_xi, couple_eta, couple_span):
    row_count = values.shape[1]
    normal_count = values.shape[3]
    grad_xi = central(padded_rows, 1, row_count)
    far_field = jnp.zeros(ghost_rows.shape, jnp.float32)
    padded_cols = jnp.concatenate([ghost_rows, values, far_field], axis=3)
    grad_eta = central(padded_cols, 3, normal_count)
    grad_span = (jnp.roll(values, -1, axis=2) - jnp.roll(values, 1, axis=2)) * 0.5
    coef_xi = advect_xi[None, :, None, :]
    coef_eta = advect_eta[None, :, None, :]
    result = -(coef_xi * grad_xi + coef_eta * grad_eta)
    result = result - couple(couple_xi, grad_xi) - couple(couple_eta, grad_eta) - couple(couple_span, grad_span)
    return result - sponge[None, :, None, :] * values


def advance(values, evaluate):
    section_one = values + time_step * evaluate(values)
    section_two = 0.75 * values + 0.25 * (section_one + time_step * evaluate(section_one))
    return values / 3.0 + 2.0 / 3.0 * (section_two + time_step * evaluate(section_two))


def reference(perturbation, advect_xi, advect_eta, sponge, couple_xi, couple_eta, couple_span, wake_cut, blowing):
    rows_all = jnp.arange(NI, dtype=jnp.int32)
    mirror_rows = NI - 1 - rows_all
    cut_rows = in_range(rows_all, wake_cut) | in_range(mirror_rows, wake_cut)
    blow_rows = blowing.astype(jnp.float32)

    def evaluate(values):
        wall_strip = values[:, :, :, :3]
        ghost_rows = wall_ghost(wall_strip, values[4, :, :, 0], blow_rows, cut_rows, wall_strip[:, ::-1])
        padded_rows = jnp.pad(values, ((0, 0), (3, 3), (0, 0), (0, 0)))
        return linear_rhs(values, ghost_rows, padded_rows, advect_xi, advect_eta, sponge, couple_xi, couple_eta, couple_span)

    values = perturbation
    for step_index in range(STEPS):
        values = advance(values, evaluate)
    return values
```

```python
import functools

import jax
import jax.numpy as jnp
from jax import lax
from jax.experimental import pallas as pl
from jax.experimental.pallas import tpu as pltpu
from jax.sharding import PartitionSpec as P

STEPS = 2
time_step = 0.2

FIELDS = 5
REACH = 9
HALO = REACH * STEPS
LANES = 256
STRIP = 32
PLANES = 4
SEGMENTS = 8

f32 = jnp.float32
bf16 = jnp.bfloat16


def iota(shape, axis):
    return lax.broadcasted_iota(jnp.int32, shape, axis)


def lane_index(shape, axis, rows):
    n = iota(shape, axis)
    own = rows * FIELDS
    h = n - own
    comp = jnp.where(n < own, n // rows, h // HALO)
    slot = jnp.where(n < own, HALO + n % rows, h % HALO)
    valid = n < own + FIELDS * HALO
    return jnp.where(valid, comp, -1), jnp.where(valid, slot, -100), n < own


def split(x):
    hi = x.astype(bf16)
    lo = (x - hi.astype(f32)).astype(bf16)
    return hi, lo


def place(values, where_from):
    return jnp.dot(values.astype(bf16), where_from.astype(bf16), preferred_element_type=f32)


def head_or_tail(is_odd, block, first):
    rows = block.shape[0]
    tail, head = block[rows - HALO:], block[:HALO]
    return jnp.where(is_odd == first, head, tail)


def wall_strips(load, count):
    lane = iota((1, 128), 1)
    out = load(0)
    for q in range(1, count):
        out = jnp.where(lane >= q * STRIP, pltpu.roll(load(q), q * STRIP, axis=1), out)
    return out


def pack_kernel(rows, me_ref, pert, ax, ae, sp, blow, mirror_out, even_out, odd_out):
    is_odd = me_ref[0] % 2
    coefs = (ax, ae, sp)
    own = rows * FIELDS
    total = own + rows
    pieces = [
        wall_strips(lambda k, c=c: pert[c, :, k, 0:128], PLANES) for c in range(FIELDS)
    ]
    pieces.append(wall_strips(lambda q: coefs[q][:, 0:128], 3))
    block = jnp.concatenate(pieces, axis=0)
    ri, ci = iota((total, total), 0), iota((total, total), 1)
    turn = ((ri // rows == ci // rows) & (ri % rows == rows - 1 - ci % rows)).astype(f32)
    mirror_out[0:total] = jnp.dot(
        turn, block, precision=lax.Precision.HIGHEST, preferred_element_type=f32
    )
    flags = jnp.broadcast_to(blow[...].astype(f32), (8, rows))
    a, b = iota((rows, 128), 0), iota((rows, 128), 1)
    mirror_out[total:total + 8] = place(flags, b == 2 * rows + rows - 1 - a)
    a, b = iota((rows, LANES), 0), iota((rows, LANES), 1)
    for out, first in ((even_out, 1), (odd_out, 0)):
        for k in range(PLANES):
            for c in range(FIELDS):
                out[k * 96 + c * HALO:k * 96 + (c + 1) * HALO] = head_or_tail(
                    is_odd, pert[c, :, k, :], first
                )
            out[k * 96 + 90:k * 96 + 96] = jnp.zeros((6, LANES), f32)
        for q in range(3):
            out[384 + q * 24:384 + q * 24 + HALO] = head_or_tail(is_odd, coefs[q][...], first)
            out[384 + q * 24 + HALO:384 + q * 24 + 24] = jnp.zeros((24 - HALO, LANES), f32)
        start = jnp.where(is_odd == first, 0, rows - HALO)
        base = own + 2 * HALO
        out[456:464] = place(flags, (b - base == a - start) & (b >= base) & (b < base + HALO))


def pack_strips_kernel(rows, me_ref, strips, even_out, odd_out):
    is_odd = me_ref[0] % 2
    own = rows * FIELDS
    b, a = iota((128, 128), 1), iota((128, 128), 0)
    for out, first in ((even_out, 1), (odd_out, 0)):
        for c in range(FIELDS):
            out[c * HALO:(c + 1) * HALO] = head_or_tail(
                is_odd, strips[c * rows:(c + 1) * rows], first
            )
        out[90:96] = jnp.zeros((6, 128), f32)
        out[96:96 + HALO] = head_or_tail(is_odd, strips[own:own + rows], first)
        out[96 + HALO:120] = jnp.zeros((24 - HALO, 128), f32)
        start = jnp.where(is_odd == first, 0, rows - HALO)
        base = own + 2 * HALO - 128
        out[120:128] = place(
            strips[own + rows:own + rows + 8],
            (b - base == a - 2 * rows - start) & (b >= base) & (b < base + HALO),
        )


def main_kernel(
    rows, total_rows, me_ref, cut_ref, cxi, ceta, cspan,
    pert, ax, ae, sp, blow, strips, even_in, odd_in, even_strips, odd_strips,
    out,
    vnat, xs, v0, xe, gs, gv, ge, rr, zz, coef, coef_e, gcoef, gcoef_e, lanes_ref,
    w1, w2, wm, wbase, ynat,
):
    me = me_ref[0]
    is_odd = me % 2
    own = rows * FIELDS
    slots = rows + HALO
    coefs_in = (ax, ae, sp)
    scales = (-time_step / 60.0, -time_step / 60.0, -time_step)
    last = pl.num_programs

    rc, rs, _ = lane_index((LANES, LANES), 0, rows)
    cc, cs, _ = lane_index((LANES, LANES), 1, rows)
    apart = jnp.where((rs >= 0) & (cs >= 0), (rs - cs + slots) % slots, 0)
    band = jnp.zeros((LANES, LANES), f32)
    for d, value in ((1, 45.0), (2, -9.0), (3, 1.0)):
        band = jnp.where(apart == d, value, band)
        band = jnp.where(apart == slots - d, -value, band)
    same = ((rs == cs) & (rs >= 0)).astype(f32)
    col_comp, _, _ = lane_index((1, LANES), 1, rows)

    def spread(matrix):
        total = jnp.zeros((LANES, LANES), f32)
        for d in range(FIELDS):
            line = jnp.zeros((1, LANES), f32)
            for c in range(FIELDS):
                line = jnp.where(col_comp == c, matrix[c, d], line)
            total = jnp.where(rc == d, line, total)
        return total

    hi, lo = split(spread(cxi) * band * (-time_step / 60.0))
    wbase[0:LANES] = hi
    wbase[LANES:2 * LANES] = lo
    wbase[2 * LANES:3 * LANES] = jnp.where(rc == cc, band, 0.0).astype(bf16)
    hi, lo = split(spread(ceta) * same * (-time_step / 60.0))
    w1[3 * LANES:4 * LANES] = hi
    w1[4 * LANES:5 * LANES] = lo
    w1[5 * LANES:6 * LANES] = hi
    hi, lo = split(spread(cspan) * same * (-time_step * 0.5))
    w2[0:LANES] = hi
    w2[LANES:2 * LANES] = lo
    w2[2 * LANES:3 * LANES] = hi

    def set_xi_weights(low, high):
        keep = jnp.where((rs >= low) & (rs < high), 0.0, 1.0).astype(bf16)
        hi, lo = wbase[0:LANES] * keep, wbase[LANES:2 * LANES] * keep
        w1[0:LANES] = hi
        w1[LANES:2 * LANES] = lo
        w1[2 * LANES:3 * LANES] = hi
        m = wbase[2 * LANES:3 * LANES] * keep
        wm[0:LANES] = m
        wm[LANES:2 * LANES] = m

    comp, slot, is_own = lane_index((1, LANES), 1, rows)
    sign = jnp.where(comp == 2, -1.0, 1.0).astype(f32)
    a, b = iota((rows, LANES), 0), iota((rows, LANES), 1)
    own_flags = place(
        jnp.broadcast_to(blow[...].astype(f32), (8, rows)), b == 2 * rows + a
    )
    own_mirror = jnp.concatenate(
        [strips[own + rows:own + rows + 8], jnp.zeros((8, LANES - 128), f32)], axis=1
    )

    def cut_lanes(g):
        i = me * rows + g - HALO
        mirror = total_rows - 1 - i
        inside = ((i >= cut_ref[0]) & (i < cut_ref[1])) | (
            (mirror >= cut_ref[0]) & (mirror < cut_ref[1])
        )
        return inside.astype(f32)

    def to_segments(natural, store):
        ynat[0] = natural[:, 0:128].T
        ynat[1] = natural[:, 128:256].T
        return ynat

    def transposed(block):
        return block.T

    def read_window(halo, halo_strips, halo_right):
        for k in range(PLANES):
            for c in range(FIELDS):
                vnat[c * rows:(c + 1) * rows] = pert[c, :, k, :]
            vnat[own:LANES] = halo[k * 96:(k + 1) * 96]
            for t in range(2):
                ynat[t] = vnat[t * 128:(t + 1) * 128].T
            for jl in range(32):
                for t in range(2):
                    xs[k, 3 + jl, :, t * 128:(t + 1) * 128] = ynat[
                        t, pl.ds(jl, SEGMENTS, stride=32), :
                    ]
        for q in range(3):
            for c in range(FIELDS):
                vnat[c * rows:(c + 1) * rows] = coefs_in[q][...]
                vnat[own + c * HALO:own + (c + 1) * HALO] = halo[
                    384 + q * 24:384 + q * 24 + HALO
                ]
            vnat[own + FIELDS * HALO:LANES] = jnp.zeros((LANES - own - FIELDS * HALO, LANES), f32)
            for t in range(2):
                ynat[t] = vnat[t * 128:(t + 1) * 128].T * scales[q]
            for jl in range(32):
                for t in range(2):
                    coef[q, jl, :, t * 128:(t + 1) * 128] = ynat[
                        t, pl.ds(jl, SEGMENTS, stride=32), :
                    ]
        vnat[0:own, 0:128] = strips[0:own]
        vnat[own:LANES, 0:128] = halo_strips[0:96]
        for t in range(2):
            ynat[t, 0:128] = vnat[t * 128:(t + 1) * 128, 0:128].T
        for m in range(HALO):
            for t in range(2):
                line = ynat[t, pl.ds(m, PLANES, stride=STRIP), :]
                gs[3 + m, 0:4, t * 128:(t + 1) * 128] = line
                gs[3 + m, 4:8, t * 128:(t + 1) * 128] = line
        for c in range(FIELDS):
            vnat[c * rows:(c + 1) * rows, 0:128] = strips[own:own + rows]
            vnat[own + c * HALO:own + (c + 1) * HALO, 0:128] = halo_strips[96:96 + HALO]
        for t in range(2):
            ynat[t, 0:128] = vnat[t * 128:(t + 1) * 128, 0:128].T
        for q in range(3):
            for m in range(HALO):
                for t in range(2):
                    gcoef[q, m, :, t * 128:(t + 1) * 128] = jnp.broadcast_to(
                        ynat[t, q * STRIP + m:q * STRIP + m + 1, :] * scales[q], (8, 128)
                    )
        g = jnp.where(is_own, slot, jnp.where(halo_right == 1, slots + slot, slot))
        lanes_ref[0] = jnp.broadcast_to(cut_lanes(g), (8, LANES))
        lanes_ref[1] = 2.0 * (own_flags + halo[456:464])
        lanes_ref[2] = 2.0 * (
            own_mirror
            + jnp.concatenate([jnp.zeros((8, 128), f32), halo_strips[120:128]], axis=1)
        )

    sub = iota((8, LANES), 0)

    def pressure(line):
        near = pltpu.roll(line, LANES - 2 * rows, axis=1)
        far = pltpu.roll(line, LANES - 2 * HALO, axis=1)
        return jnp.where(is_own, near, far)

    def slopes(load, offset):
        return (
            45.0 * (load(offset + 1) - load(offset - 1))
            - 9.0 * (load(offset + 2) - load(offset - 2))
            + (load(offset + 3) - load(offset - 3))
        )

    def time_stage(depth, alpha, beta):
        cut = lanes_ref[0] > 0.5
        wall = []
        for m in range(3):
            line = jnp.concatenate([xs[k, 3 + m, 0:1, :] for k in range(PLANES)], axis=0)
            wall.append(jnp.concatenate([line, line], axis=0))
        wall_g = [gs[3 + m] for m in range(3)]
        lift = lanes_ref[1] * jnp.where(comp == 2, pressure(wall[0]), 0.0)
        lift_g = lanes_ref[2] * jnp.where(comp == 2, pressure(wall_g[0]), 0.0)
        for m in range(3):
            ghost = jnp.where(cut, sign * wall_g[m], sign * wall[m] + lift)
            gs[2 - m] = jnp.where(cut, sign * wall[m], sign * wall_g[m] + lift_g)
            for k in range(PLANES):
                below = pltpu.roll(xs[k, 34 - m], 1, axis=0)
                xs[k, 2 - m] = jnp.where(sub == 0, ghost[k:k + 1], below)
                above = pltpu.roll(xs[k, 3 + m], SEGMENTS - 1, axis=0)
                xs[k, 35 + m] = jnp.where(sub == SEGMENTS - 1, 0.0, above)
        for k in range(PLANES):
            x = xs[k, 3:35].reshape(LANES, LANES)
            e = slopes(lambda at: xs[k, at:at + 32], 3).reshape(LANES, LANES)
            xh, xl = split(x)
            eh, el = split(e)
            first = jnp.dot(
                jnp.concatenate([xh, xh, xl, eh, eh, el], axis=1), w1[...],
                preferred_element_type=f32,
            )
            grad = jnp.dot(
                jnp.concatenate([xh, xl], axis=1), wm[...], preferred_element_type=f32
            )
            zz[k] = jnp.dot(
                jnp.concatenate([xh, xh, xl], axis=1), w2[...], preferred_element_type=f32
            )
            ca = coef[0].reshape(LANES, LANES)
            cb = coef[1].reshape(LANES, LANES)
            cd = coef[2].reshape(LANES, LANES)
            rr[k] = first + ca * grad + cb * e + cd * x
        n = depth * 8
        x = gs[3:3 + depth].reshape(n, LANES)
        e = slopes(lambda at: gs[at:at + depth], 3).reshape(n, LANES)
        xh, xl = split(x)
        eh, el = split(e)
        first = jnp.dot(
            jnp.concatenate([-xh, -xh, -xl, eh, eh, el], axis=1), w1[...],
            preferred_element_type=f32,
        )
        grad = jnp.dot(
            jnp.concatenate([-xh, -xl], axis=1), wm[...], preferred_element_type=f32
        )
        z = jnp.dot(
            jnp.concatenate([xh, xh, xl], axis=1), w2[...], preferred_element_type=f32
        ).reshape(depth, 8, LANES)
        span = pltpu.roll(z, 7, axis=1) - pltpu.roll(z, 1, axis=1)
        ca, cb, cd = (gcoef[q, 0:depth].reshape(n, LANES) for q in range(3))
        r = (first + ca * grad + cb * e + cd * x).reshape(depth, 8, LANES) + span
        gs[3:3 + depth] = alpha * gv[0:depth] + beta * (gs[3:3 + depth] + r)
        for k in range(PLANES):
            r = rr[k] + (zz[(k + 1) % PLANES] - zz[(k - 1) % PLANES])
            x = xs[k, 3:35] + r.reshape(32, 8, LANES)
            xs[k, 3:35] = alpha * v0[k] + beta * x

    def time_steps(depth):
        for k in range(PLANES):
            v0[k] = xs[k, 3:35]
        gv[0:depth] = gs[3:3 + depth]

        def stage(s, carry):
            alpha = jnp.where(s == 0, 0.0, jnp.where(s == 1, 0.75, 1.0 / 3.0)).astype(f32)
            beta = jnp.where(s == 0, 1.0, jnp.where(s == 1, 0.25, 2.0 / 3.0)).astype(f32)
            time_stage(depth, alpha, beta)
            return carry

        lax.fori_loop(0, 3, stage, 0)

    at_start = me == 0
    at_end = me == total_rows // rows - 1
    gs[...] = jnp.zeros(gs.shape, f32)
    set_xi_weights(0, 0)
    read_window(even_in, even_strips, 1 - is_odd)
    time_steps(HALO - 3)
    for k in range(PLANES):
        xe[k] = xs[k, 3:35]
    ge[...] = gs[3:3 + REACH]
    coef_e[...] = coef[...]
    gcoef_e[...] = gcoef[:, 0:REACH]
    blow_e, blow_ge = lanes_ref[1], lanes_ref[2]
    outside = at_start | at_end
    set_xi_weights(0, jnp.where(outside, HALO, 0))
    read_window(odd_in, odd_strips, is_odd)
    time_steps(HALO - 3)
    set_xi_weights(
        jnp.where(at_start, REACH, 0),
        jnp.where(at_start, HALO, jnp.where(at_end, REACH, 0)),
    )
    left = (slot >= REACH) & (slot < REACH + rows)
    from_e = jnp.where(left, is_odd, 1 - is_odd) == 1
    for k in range(PLANES):
        xs[k, 3:35] = jnp.where(from_e, xe[k], xs[k, 3:35])
    gs[3:3 + REACH] = jnp.where(from_e, ge[...], gs[3:3 + REACH])
    coef[...] = jnp.where(from_e, coef_e[...], coef[...])
    gcoef[:, 0:REACH] = jnp.where(from_e, gcoef_e[...], gcoef[:, 0:REACH])
    g = jnp.where(is_own, slot, jnp.where(slot < REACH, slots + slot, slot))
    lanes_ref[0] = jnp.broadcast_to(cut_lanes(g), (8, LANES))
    lanes_ref[1] = jnp.where(from_e, blow_e, lanes_ref[1])
    lanes_ref[2] = jnp.where(from_e, blow_ge, lanes_ref[2])
    time_steps(REACH - 3)
    for k in range(PLANES):
        for jl in range(32):
            for t in range(2):
                ynat[t, pl.ds(jl, SEGMENTS, stride=32), :] = xs[
                    k, 3 + jl, :, t * 128:(t + 1) * 128
                ]
        low, high = ynat[0].T, ynat[1].T
        for c in range(FIELDS):
            at = c * rows
            out[c, :, k, :] = low[at:at + rows] if at < 128 else high[at - 128:at - 128 + rows]


def on_device(
    perturbation, advect_xi, advect_eta, sponge,
    couple_xi, couple_eta, couple_span, wake_cut, blowing,
):
    rows = perturbation.shape[1]
    devices = lax.axis_size("wrap")
    total_rows = rows * devices
    own = rows * FIELDS
    me = lax.axis_index("wrap").astype(jnp.int32).reshape(1)
    flags = blowing.reshape(1, rows)
    mirror = [(i, devices - 1 - i) for i in range(devices)]
    same_chip = [(i, i ^ 1) for i in range(devices)]
    next_chip = [(i, i + 1 if i % 2 else i - 1) for i in range(1, devices - 1)]

    vmem = pl.BlockSpec(memory_space=pltpu.VMEM)
    smem = pl.BlockSpec(memory_space=pltpu.SMEM)
    params = pltpu.CompilerParams(vmem_limit_bytes=48 * 1024 * 1024)

    def shape(*dims):
        return jax.ShapeDtypeStruct(dims, f32)

    to_mirror, to_same, to_next = pl.pallas_call(
        functools.partial(pack_kernel, rows),
        out_shape=(shape(own + rows + 8, 128), shape(464, LANES), shape(464, LANES)),
        in_specs=[smem] + [vmem] * 5,
        out_specs=(vmem,) * 3,
        compiler_params=params,
    )(me, perturbation, advect_xi, advect_eta, sponge, flags)

    strips = lax.ppermute(to_mirror, "wrap", mirror)
    from_same = lax.ppermute(to_same, "wrap", same_chip)
    from_next = lax.ppermute(to_next, "wrap", next_chip)

    strip_same, strip_next = pl.pallas_call(
        functools.partial(pack_strips_kernel, rows),
        out_shape=(shape(128, 128), shape(128, 128)),
        in_specs=[smem, vmem],
        out_specs=(vmem,) * 2,
        compiler_params=params,
    )(me, strips)
    strips_same = lax.ppermute(strip_same, "wrap", same_chip)
    strips_next = lax.ppermute(strip_next, "wrap", next_chip)

    state = (PLANES, 32, SEGMENTS, LANES)
    scratch = [
        pltpu.VMEM((LANES, LANES), f32),
        pltpu.VMEM((PLANES, 38, SEGMENTS, LANES), f32),
        pltpu.VMEM(state, f32),
        pltpu.VMEM(state, f32),
        pltpu.VMEM((3 + HALO + 3, 8, LANES), f32),
        pltpu.VMEM((HALO, 8, LANES), f32),
        pltpu.VMEM((REACH, 8, LANES), f32),
        pltpu.VMEM((PLANES, LANES, LANES), f32),
        pltpu.VMEM((PLANES, LANES, LANES), f32),
        pltpu.VMEM((3, 32, SEGMENTS, LANES), f32),
        pltpu.VMEM((3, 32, SEGMENTS, LANES), f32),
        pltpu.VMEM((3, HALO, 8, LANES), f32),
        pltpu.VMEM((3, REACH, 8, LANES), f32),
        pltpu.VMEM((3, 8, LANES), f32),
        pltpu.VMEM((6 * LANES, LANES), bf16),
        pltpu.VMEM((3 * LANES, LANES), bf16),
        pltpu.VMEM((2 * LANES, LANES), bf16),
        pltpu.VMEM((3 * LANES, LANES), bf16),
        pltpu.VMEM((2, LANES, 128), f32),
    ]
    return pl.pallas_call(
        functools.partial(main_kernel, rows, total_rows),
        out_shape=shape(*perturbation.shape),
        in_specs=[smem] * 5 + [vmem] * 10,
        out_specs=vmem,
        scratch_shapes=scratch,
        compiler_params=params,
    )(
        me, wake_cut, couple_xi, couple_eta, couple_span,
        perturbation, advect_xi, advect_eta, sponge, flags,
        strips, from_same, from_next, strips_same, strips_next,
    )


def solution(mesh):
    in_specs = (
        P(None, "wrap", None, None),
        P("wrap", None),
        P("wrap", None),
        P("wrap", None),
        P(),
        P(),
        P(),
        P(),
        P("wrap"),
    )
    out_specs = P(None, "wrap", None, None)
    return jax.shard_map(
        on_device, mesh=mesh, in_specs=in_specs, out_specs=out_specs, check_vma=False
    )
```

```python
import functools

import jax
import jax.numpy as jnp
from jax import lax
from jax.experimental import pallas as pl
from jax.experimental.pallas import tpu as pltpu
from jax.sharding import PartitionSpec as P

STEPS = 2
time_step = 0.2

FIELDS = 5
REACH = 9
HALO = REACH * STEPS
LANES = 256
STRIP = 32
PLANES = 4
SEGMENTS = 8

PAYLOAD = 464
SCALES = (-time_step / 60.0, -time_step * 45.0 / 60.0, -time_step)
KEEPS = (0.0, 0.0, 1.0)

f32 = jnp.float32
bf16 = jnp.bfloat16
f8 = jnp.float8_e5m2

HELD = 16.0


def iota(shape, axis):
    return lax.broadcasted_iota(jnp.int32, shape, axis)


def lane_index(shape, axis, rows):
    n = iota(shape, axis)
    own = rows * FIELDS
    h = n - own
    comp = jnp.where(n < own, n // rows, h // HALO)
    slot = jnp.where(n < own, HALO + n % rows, h % HALO)
    valid = n < own + FIELDS * HALO
    return jnp.where(valid, comp, -1), jnp.where(valid, slot, -100), n < own


def split(x):
    hi = x.astype(bf16)
    lo = (x - hi.astype(f32)).astype(bf16)
    return hi, lo


def split_small(x):
    hi = x.astype(bf16)
    return hi, (x - hi.astype(f32)).astype(f8)


def place(values, where_from):
    return jnp.dot(values.astype(bf16), where_from.astype(bf16), preferred_element_type=f32)


def head_or_tail(is_odd, block, first):
    rows = block.shape[0]
    tail, head = block[rows - HALO:], block[:HALO]
    return jnp.where(is_odd == first, head, tail)


def wall_strips(load, count):
    lane = iota((1, 128), 1)
    out = load(0)
    for q in range(1, count):
        out = jnp.where(lane >= q * STRIP, pltpu.roll(load(q), q * STRIP, axis=1), out)
    return out


def pack_mirror_kernel(
    rows, pert_hbm, ax_hbm, ae_hbm, sp_hbm, blow, mirror_out, pert, coefs, sems
):
    near = pl.ds(0, 128)
    copies = [pltpu.make_async_copy(pert_hbm.at[:, :, :, near], pert, sems.at[0])]
    for q, ref in enumerate((ax_hbm, ae_hbm, sp_hbm)):
        copies.append(pltpu.make_async_copy(ref.at[:, near], coefs.at[q], sems.at[1 + q]))
    for copy in copies:
        copy.start()
    own = rows * FIELDS
    total = own + rows
    ri, ci = iota((total, total), 0), iota((total, total), 1)
    turn = ((ri // rows == ci // rows) & (ri % rows == rows - 1 - ci % rows)).astype(f32)
    turn = turn * jnp.where(ci < own, HELD, 1.0)
    flags = jnp.broadcast_to(blow[...].astype(f32), (8, rows))
    a, b = iota((rows, 128), 0), iota((rows, 128), 1)
    mirror_out[total:total + 8] = place(flags, b == 2 * rows + rows - 1 - a)
    for copy in copies:
        copy.wait()
    pieces = [
        wall_strips(lambda k, c=c: pert[c, :, k, :], PLANES) for c in range(FIELDS)
    ]
    pieces.append(wall_strips(lambda q: coefs[q], 3))
    mirror_out[0:total] = jnp.dot(
        turn, jnp.concatenate(pieces, axis=0),
        precision=lax.Precision.HIGHEST, preferred_element_type=f32,
    )


def pack_strips_kernel(
    rows, me_ref, strips, even_in, odd_in, even_out, odd_out, stage, sems
):
    is_odd = me_ref[0] % 2
    own = rows * FIELDS
    b, a = iota((128, 128), 1), iota((128, 128), 0)
    copies = []
    for p, (out, first) in enumerate(((even_out, 1), (odd_out, 0))):
        parts = [
            head_or_tail(is_odd, strips[c * rows:(c + 1) * rows], first)
            for c in range(FIELDS)
        ]
        parts.append(jnp.zeros((6, 128), f32))
        parts.append(head_or_tail(is_odd, strips[own:own + rows], first))
        parts.append(jnp.zeros((24 - HALO, 128), f32))
        start = jnp.where(is_odd == first, 0, rows - HALO)
        base = own + 2 * HALO - 128
        parts.append(place(
            strips[own + rows:own + rows + 8],
            (b - base == a - 2 * rows - start) & (b >= base) & (b < base + HALO),
        ))
        block = jnp.concatenate(parts, axis=0)
        stage[p, :, 0:128] = block[0:64]
        stage[p, :, 128:256] = block[64:128]
        copy = pltpu.make_async_copy(
            stage.at[p], out.at[pl.ds(PAYLOAD, 64)], sems.at[p]
        )
        copy.start()
        copies.append(copy)
    for copy in copies:
        copy.wait()


def segments(block, hold, store):
    hold[...] = block.T
    for jl in range(32):
        store(jl, hold[pl.ds(jl, SEGMENTS, stride=32), :])


def prepare_kernel(
    rows, me_ref, cxi, ceta, cspan, pert_hbm, ax_hbm, ae_hbm, sp_hbm, blow,
    even_out, odd_out, xt, ct, last_field, wide, narrow,
    pert, coefs, hold, sems,
):
    is_odd = me_ref[0] % 2
    copies = [pltpu.make_async_copy(pert_hbm, pert, sems.at[0])]
    for q, ref in enumerate((ax_hbm, ae_hbm, sp_hbm)):
        copies.append(pltpu.make_async_copy(ref, coefs.at[q], sems.at[1 + q]))
    for copy in copies:
        copy.start()
    own = rows * FIELDS
    slots = rows + HALO
    rc, rs, _ = lane_index((LANES, LANES), 0, rows)
    cc, cs, _ = lane_index((LANES, LANES), 1, rows)
    apart = jnp.where((rs >= 0) & (cs >= 0), (rs - cs + slots) % slots, 0)
    band = jnp.zeros((LANES, LANES), f32)
    for d, value in ((1, 45.0), (2, -9.0), (3, 1.0)):
        band = jnp.where(apart == d, value, band)
        band = jnp.where(apart == slots - d, -value, band)
    same = ((rs == cs) & (rs >= 0)).astype(f32)
    col_comp, _, _ = lane_index((1, LANES), 1, rows)

    def spread(matrix):
        total = jnp.zeros((LANES, LANES), f32)
        for d in range(FIELDS):
            line = jnp.zeros((1, LANES), f32)
            for c in range(FIELDS):
                line = jnp.where(col_comp == c, matrix[c, d], line)
            total = jnp.where(rc == d, line, total)
        return total

    xi = spread(cxi) * band * (-time_step / 60.0)
    eta = spread(ceta) * same * (-time_step * 45.0 / 60.0)
    span = spread(cspan) * same * (-time_step * 0.5)
    grad = jnp.where(rc == cc, band, 0.0)
    for w, first, small in ((xi, 0, 0), (eta, 2, 1), (grad, 4, 2), (span, 5, 3)):
        hi, lo = split(w)
        wide[first * LANES:(first + 1) * LANES] = hi
        if first != 4:
            wide[(first + 1) * LANES:(first + 2) * LANES] = lo
        narrow[small * LANES:(small + 1) * LANES] = w.astype(f8)
    for copy in copies:
        copy.wait()
    a, b = iota((rows, LANES), 0), iota((rows, LANES), 1)
    flags = jnp.broadcast_to(blow[...].astype(f32), (8, rows))
    for out, first in ((even_out, 1), (odd_out, 0)):
        for k in range(PLANES):
            for c in range(FIELDS):
                out[k * 96 + c * HALO:k * 96 + (c + 1) * HALO] = head_or_tail(
                    is_odd, pert[c, :, k, :], first
                ) * HELD
            out[k * 96 + 90:k * 96 + 96] = jnp.zeros((6, LANES), f32)
        for q in range(3):
            out[384 + q * 24:384 + q * 24 + HALO] = head_or_tail(is_odd, coefs[q], first)
            out[384 + q * 24 + HALO:384 + q * 24 + 24] = jnp.zeros((24 - HALO, LANES), f32)
        start = jnp.where(is_odd == first, 0, rows - HALO)
        base = own + 2 * HALO
        out[456:464] = place(flags, (b - base == a - start) & (b >= base) & (b < base + HALO))
        out[PAYLOAD:PAYLOAD + 64] = jnp.zeros((64, LANES), f32)
    for k in range(PLANES):
        block = HELD * jnp.concatenate([pert[c, :, k, :] for c in range(FIELDS - 1)], axis=0)

        def store(jl, slab, k=k):
            xt[k, jl] = slab

        segments(block, hold, store)
        last_field[k] = pert[FIELDS - 1, :, k, :] * HELD
    for q in range(3):
        block = jnp.concatenate([coefs[q] * SCALES[q] + KEEPS[q]] * (FIELDS - 1), axis=0)

        def store(jl, slab, q=q):
            ct[q, jl] = slab

        segments(block, hold, store)


def window_kernel(
    rows, total_rows, second, me_ref, cut_ref, blow, strips, xt, ct, last_field,
    wide, narrow, halo_in, *rest,
):
    if second:
        xe, ge, ce, gce, le = rest[:5]
        out, rest = rest[5], rest[6:]
    else:
        xe, ge, ce, gce, le = rest[:5]
        rest = rest[5:]
    (
        xs, v0, gs, gv, zz, partial, high, low, span_high, span_low,
        coef, gcoef, lanes_ref, wx, wx8, hold,
    ) = rest
    me = me_ref[0]
    is_odd = me % 2
    own = rows * FIELDS
    slots = rows + HALO
    rs = lane_index((LANES, LANES), 0, rows)[1]

    def set_xi_weights(low, high):
        keep = jnp.where((rs >= low) & (rs < high), 0.0, 1.0)
        for source, kept, count, masked in (
            (wide, wx, 7, (0, 1, 4)), (narrow, wx8, 4, (0, 2)),
        ):
            for t in range(count):
                block = source[t * LANES:(t + 1) * LANES]
                if t in masked:
                    block = (block.astype(f32) * keep).astype(block.dtype)
                kept[t * LANES:(t + 1) * LANES] = block

    def dot(a, w):
        return jnp.dot(a, w, preferred_element_type=f32)

    def twice(a):
        return jnp.concatenate([a, a], axis=1)

    def couple_ij(xh, eh, low):
        n = LANES
        first = dot(jnp.concatenate([xh, xh, eh, eh], axis=1), wx[0:4 * n])
        first8 = dot(low, wx8[0:2 * n])
        grad = dot(xh, wx[4 * n:5 * n])
        grad8 = dot(low[:, 0:n], wx8[2 * n:3 * n])
        return first, first8, grad, grad8

    def couple_k(sh, sl):
        n = LANES
        return dot(twice(sh), wx[5 * n:7 * n]) + dot(sl, wx8[3 * n:4 * n])

    comp, slot, is_own = lane_index((1, LANES), 1, rows)
    sign = jnp.where(comp == 2, -1.0, 1.0).astype(f32)
    a, b = iota((rows, LANES), 0), iota((rows, LANES), 1)
    own_flags = place(
        jnp.broadcast_to(blow[...].astype(f32), (8, rows)), b == 2 * rows + a
    )
    own_mirror = jnp.concatenate(
        [strips[own + rows:own + rows + 8], jnp.zeros((8, LANES - 128), f32)], axis=1
    )

    def cut_lanes(g):
        i = me * rows + g - HALO
        mirror = total_rows - 1 - i
        inside = ((i >= cut_ref[0]) & (i < cut_ref[1])) | (
            (mirror >= cut_ref[0]) & (mirror < cut_ref[1])
        )
        return inside.astype(f32)

    def read_window(halo, halo_right):
        for k in range(PLANES):
            xs[k, 3:35, :, 0:128] = xt[k]

            def store(jl, slab, k=k):
                xs[k, 3 + jl, :, 128:256] = slab

            segments(
                jnp.concatenate([last_field[k], halo[k * 96:(k + 1) * 96]], axis=0),
                hold, store,
            )
        for q in range(3):
            coef[q, :, :, 0:128] = ct[q]
            edge = halo[384 + q * 24:384 + q * 24 + HALO] * SCALES[q] + KEEPS[q]
            block = jnp.concatenate(
                [jnp.zeros((rows, LANES), f32)] + [edge] * FIELDS
                + [jnp.zeros((128 - rows - FIELDS * HALO, LANES), f32)], axis=0,
            )
            lane = iota((1, 128), 1)

            def store(jl, slab, q=q):
                coef[q, jl, :, 128:256] = jnp.where(lane < rows, ct[q, jl], slab)

            segments(block, hold, store)
        near, far = halo[PAYLOAD:PAYLOAD + 64, 0:128], halo[PAYLOAD:PAYLOAD + 64, 128:256]
        last = strips[(FIELDS - 1) * rows:own]
        left = strips[0:128].T
        right = jnp.concatenate([last, near, far[0:32]], axis=0).T
        hold[0:128], hold[128:256] = left, right
        for m in range(HALO):
            for t in range(2):
                line = hold[pl.ds(t * 128 + m, PLANES, stride=STRIP), :]
                gs[3 + m, 0:4, t * 128:(t + 1) * 128] = line
                gs[3 + m, 4:8, t * 128:(t + 1) * 128] = line
        mine, edge = strips[own:own + rows], far[32:32 + HALO]
        hold[0:128] = jnp.concatenate([mine] * (FIELDS - 1), axis=0).T
        hold[128:256] = jnp.concatenate(
            [mine] + [edge] * FIELDS
            + [jnp.zeros((128 - rows - FIELDS * HALO, 128), f32)], axis=0,
        ).T
        for q in range(3):
            for m in range(HALO):
                for t in range(2):
                    at = t * 128 + q * STRIP + m
                    gcoef[q, m, :, t * 128:(t + 1) * 128] = jnp.broadcast_to(
                        hold[at:at + 1, :] * SCALES[q] + KEEPS[q], (8, 128)
                    )
        g = jnp.where(is_own, slot, jnp.where(halo_right == 1, slots + slot, slot))
        lanes_ref[0] = jnp.broadcast_to(cut_lanes(g), (8, LANES))
        lanes_ref[1] = 2.0 * (own_flags + halo[456:464])
        lanes_ref[2] = 2.0 * (
            own_mirror + jnp.concatenate([jnp.zeros((8, 128), f32), far[56:64]], axis=1)
        )

    sub = iota((8, LANES), 0)

    def pressure(line):
        near = pltpu.roll(line, LANES - 2 * rows, axis=1)
        far = pltpu.roll(line, LANES - 2 * HALO, axis=1)
        return jnp.where(is_own, near, far)

    def slopes(load, offset):
        return (
            (load(offset + 1) - load(offset - 1))
            - 0.2 * (load(offset + 2) - load(offset - 2))
            + (1.0 / 45.0) * (load(offset + 3) - load(offset - 3))
        )

    def time_stage(depth, alpha, beta):
        cut = lanes_ref[0] > 0.5
        wall = []
        for m in range(3):
            line = jnp.concatenate([xs[k, 3 + m, 0:1, :] for k in range(PLANES)], axis=0)
            wall.append(jnp.concatenate([line, line], axis=0))
        wall_g = [gs[3 + m] for m in range(3)]
        lift = lanes_ref[1] * jnp.where(comp == 2, pressure(wall[0]), 0.0)
        lift_g = lanes_ref[2] * jnp.where(comp == 2, pressure(wall_g[0]), 0.0)
        for m in range(3):
            ghost = jnp.where(cut, sign * wall_g[m], sign * wall[m] + lift)
            gs[2 - m] = jnp.where(cut, sign * wall[m], sign * wall_g[m] + lift_g)
            for k in range(PLANES):
                below = pltpu.roll(xs[k, 34 - m], 1, axis=0)
                xs[k, 2 - m] = jnp.where(sub == 0, ghost[k:k + 1], below)
                above = pltpu.roll(xs[k, 3 + m], SEGMENTS - 1, axis=0)
                xs[k, 35 + m] = jnp.where(sub == SEGMENTS - 1, 0.0, above)
        rows8 = 8 * SEGMENTS
        chunks = [(8 * c, slice(rows8 * c, rows8 * (c + 1))) for c in range(4)]

        def flat(v):
            return v.reshape(rows8, LANES)

        def split_plane(k):
            for at, here in chunks:
                x = flat(xs[k, 3 + at:11 + at])
                e = flat(slopes(lambda o: xs[k, at + o:at + o + 8], 3))
                cb, cd = flat(coef[1, at:at + 8]), flat(coef[2, at:at + 8])
                partial[k, here] = cb * e + cd * x
                xh, xl = split_small(x)
                eh, el = split_small(e)
                high[k, here, 0:LANES] = xh
                high[k, here, LANES:2 * LANES] = eh
                low[k, here, 0:LANES] = xl
                low[k, here, LANES:2 * LANES] = el

        for p in range(2):
            for at, here in chunks:
                s = xs[p + 1, 3 + at:11 + at] - xs[(p + 3) % PLANES, 3 + at:11 + at]
                span_high[p, here], span_low[p, here] = split_small(flat(s))
        split_plane(0)
        for p in range(2):
            zz[p] = couple_k(span_high[p], span_low[p])
        for k in range(PLANES):
            first, first8, grad, grad8 = couple_ij(
                high[k, :, 0:LANES], high[k, :, LANES:2 * LANES], low[k]
            )
            if k + 1 < PLANES:
                split_plane(k + 1)
            for at, here in chunks:
                ca = flat(coef[0, at:at + 8])
                r = (first[here] + first8[here]) + ca * (grad[here] + grad8[here])
                r = r + partial[k, here]
                r = r + zz[k, here] if k < 2 else r - zz[k - 2, here]
                r = alpha * flat(v0[k, at:at + 8]) + beta * r
                xs[k, 3 + at:11 + at] = r.reshape(8, SEGMENTS, LANES)
        n = depth * 8
        x = gs[3:3 + depth].reshape(n, LANES)
        e = slopes(lambda at: gs[at:at + depth], 3).reshape(n, LANES)
        xh, xl = split_small(x)
        eh, el = split_small(-e)
        first, first8, grad, grad8 = couple_ij(xh, eh, jnp.concatenate([xl, el], axis=1))
        s = gs[3:3 + depth]
        s = pltpu.roll(s, 7, axis=1) - pltpu.roll(s, 1, axis=1)
        z = couple_k(*split_small(s.reshape(n, LANES)))
        ca, cb, cd = (gcoef[q, 0:depth].reshape(n, LANES) for q in range(3))
        r = cb * e + cd * x - (first + first8) - ca * (grad + grad8) + z
        gs[3:3 + depth] = alpha * gv[0:depth] + beta * r.reshape(depth, 8, LANES)

    def time_steps(depth):
        for k in range(PLANES):
            v0[k] = xs[k, 3:35]
        gv[0:depth] = gs[3:3 + depth]

        def stage(s, carry):
            alpha = jnp.where(s == 0, 0.0, jnp.where(s == 1, 0.75, 1.0 / 3.0)).astype(f32)
            beta = jnp.where(s == 0, 1.0, jnp.where(s == 1, 0.25, 2.0 / 3.0)).astype(f32)
            time_stage(depth, alpha, beta)
            return carry

        lax.fori_loop(0, 3, stage, 0)

    at_start = me == 0
    at_end = me == total_rows // rows - 1
    gs[...] = jnp.zeros(gs.shape, f32)
    if not second:
        set_xi_weights(0, 0)
        read_window(halo_in, 1 - is_odd)
        time_steps(HALO - 2)
        for k in range(PLANES):
            xe[k] = xs[k, 3:35]
        ge[...] = gs[3:3 + REACH]
        for q in range(3):
            ce[q] = coef[q, :, :, 128:256]
        gce[...] = gcoef[:, 0:REACH]
        le[...] = lanes_ref[...]
        return
    outside = at_start | at_end
    set_xi_weights(0, jnp.where(outside, HALO, 0))
    read_window(halo_in, is_odd)
    time_steps(HALO - 2)
    set_xi_weights(
        jnp.where(at_start, REACH, 0),
        jnp.where(at_start, HALO, jnp.where(at_end, REACH, 0)),
    )
    left = (slot >= REACH) & (slot < REACH + rows)
    from_e = jnp.where(left, is_odd, 1 - is_odd) == 1
    for k in range(PLANES):
        xs[k, 3:35] = jnp.where(from_e, xe[k], xs[k, 3:35])
    gs[3:3 + REACH] = jnp.where(from_e, ge[...], gs[3:3 + REACH])
    coef[:, :, :, 128:256] = jnp.where(from_e[:, 128:256], ce[...], coef[:, :, :, 128:256])
    gcoef[:, 0:REACH] = jnp.where(from_e, gce[...], gcoef[:, 0:REACH])
    g = jnp.where(is_own, slot, jnp.where(slot < REACH, slots + slot, slot))
    lanes_ref[0] = jnp.broadcast_to(cut_lanes(g), (8, LANES))
    lanes_ref[1] = jnp.where(from_e, le[1], lanes_ref[1])
    lanes_ref[2] = jnp.where(from_e, le[2], lanes_ref[2])
    time_steps(REACH - 1)
    for k in range(PLANES):
        for t in range(2):
            for jl in range(32):
                hold[pl.ds(jl, SEGMENTS, stride=32), :] = xs[
                    k, 3 + jl, :, t * 128:(t + 1) * 128
                ]
            block = hold[...].T * (1.0 / HELD)
            for c in range(FIELDS):
                at = c * rows - t * 128
                if 0 <= at < 128:
                    out[c, :, k, :] = block[at:at + rows]


def on_device(
    perturbation, advect_xi, advect_eta, sponge,
    couple_xi, couple_eta, couple_span, wake_cut, blowing,
):
    rows = perturbation.shape[1]
    devices = lax.axis_size("wrap")
    total_rows = rows * devices
    own = rows * FIELDS
    me = lax.axis_index("wrap").astype(jnp.int32).reshape(1)
    flags = blowing.reshape(1, rows)
    mirror = [(i, devices - 1 - i) for i in range(devices)]
    same_chip = [(i, i ^ 1) for i in range(devices)]
    next_chip = [(i, i + 1 if i % 2 else i - 1) for i in range(1, devices - 1)]

    vmem = pl.BlockSpec(memory_space=pltpu.VMEM)
    smem = pl.BlockSpec(memory_space=pltpu.SMEM)
    anywhere = pl.BlockSpec(memory_space=pl.ANY)
    hbm = pl.BlockSpec(memory_space=pltpu.HBM)

    def call(kernel, outs, ins, scratch, us, out_specs=None, vmem_kib=32 * 1024, **more):
        return pl.pallas_call(
            kernel,
            out_shape=outs,
            in_specs=ins,
            out_specs=out_specs or (vmem,) * len(outs),
            scratch_shapes=scratch,
            compiler_params=pltpu.CompilerParams(vmem_limit_bytes=vmem_kib * 1024),
            cost_estimate=pl.CostEstimate(
                flops=int(us * 1e9), bytes_accessed=int(us * 3e6), transcendentals=0
            ),
            **more,
        )

    def shape(*dims, dtype=f32):
        return jax.ShapeDtypeStruct(dims, dtype)

    dma = pltpu.SemaphoreType.DMA
    (to_mirror,) = call(
        functools.partial(pack_mirror_kernel, rows),
        (shape(own + rows + 8, 128),),
        [hbm] * 4 + [vmem],
        [
            pltpu.VMEM((FIELDS, rows, PLANES, 128), f32),
            pltpu.VMEM((3, rows, 128), f32),
            dma((4,)),
        ],
        1,
        vmem_kib=65340,
    )(perturbation, advect_xi, advect_eta, sponge, flags)
    strips = lax.ppermute(to_mirror, "wrap", mirror)

    state = (PLANES, 32, SEGMENTS, LANES)
    payload = shape(PAYLOAD + 64, LANES)
    even, odd, xt, ct, last_field, wide, narrow = call(
        functools.partial(prepare_kernel, rows),
        (
            payload, payload,
            shape(PLANES, 32, SEGMENTS, 128), shape(3, 32, SEGMENTS, 128),
            shape(PLANES, rows, LANES),
            shape(7 * LANES, LANES, dtype=bf16), shape(4 * LANES, LANES, dtype=f8),
        ),
        [smem] * 4 + [hbm] * 4 + [vmem],
        [
            pltpu.VMEM((FIELDS, rows, PLANES, LANES), f32),
            pltpu.VMEM((3, rows, LANES), f32),
            pltpu.VMEM((LANES, 128), f32),
            dma((4,)),
        ],
        4,
    )(
        me, couple_xi, couple_eta, couple_span,
        perturbation, advect_xi, advect_eta, sponge, flags,
    )
    even, odd = call(
        functools.partial(pack_strips_kernel, rows),
        (payload, payload),
        [smem, vmem, anywhere, anywhere],
        [pltpu.VMEM((2, 64, LANES), f32), dma((2,))],
        1,
        out_specs=(anywhere, anywhere),
        input_output_aliases={2: 0, 3: 1},
    )(me, strips, even, odd)
    from_next = lax.ppermute(odd, "wrap", next_chip)
    from_same = lax.ppermute(even, "wrap", same_chip)

    scratch = [
        pltpu.VMEM((PLANES, 38, SEGMENTS, LANES), f32),
        pltpu.VMEM(state, f32),
        pltpu.VMEM((3 + HALO + 3, 8, LANES), f32),
        pltpu.VMEM((HALO, 8, LANES), f32),
        pltpu.VMEM((2, LANES, LANES), f32),
        pltpu.VMEM((PLANES, LANES, LANES), f32),
        pltpu.VMEM((PLANES, LANES, 2 * LANES), bf16),
        pltpu.VMEM((PLANES, LANES, 2 * LANES), f8),
        pltpu.VMEM((2, LANES, LANES), bf16),
        pltpu.VMEM((2, LANES, LANES), f8),
        pltpu.VMEM((3, 32, SEGMENTS, LANES), f32),
        pltpu.VMEM((3, HALO, 8, LANES), f32),
        pltpu.VMEM((3, 8, LANES), f32),
        pltpu.VMEM((7 * LANES, LANES), bf16),
        pltpu.VMEM((4 * LANES, LANES), f8),
        pltpu.VMEM((LANES, 128), f32),
    ]
    common = (me, wake_cut, flags, strips, xt, ct, last_field, wide, narrow)
    specs = [smem, smem] + [vmem] * 7
    first = call(
        functools.partial(window_kernel, rows, total_rows, False),
        (
            shape(*state), shape(REACH, 8, LANES), shape(3, 32, SEGMENTS, 128),
            shape(3, REACH, 8, LANES), shape(3, 8, LANES),
        ),
        specs + [vmem], scratch, 9,
    )(*common, from_same)
    (out,) = call(
        functools.partial(window_kernel, rows, total_rows, True),
        (shape(*perturbation.shape),),
        specs + [vmem] * 6, scratch, 18,
    )(*common, from_next, *first)
    return out


def solution(mesh):
    in_specs = (
        P(None, "wrap", None, None),
        P("wrap", None),
        P("wrap", None),
        P("wrap", None),
        P(),
        P(),
        P(),
        P(),
        P("wrap"),
    )
    out_specs = P(None, "wrap", None, None)
    return jax.shard_map(
        on_device, mesh=mesh, in_specs=in_specs, out_specs=out_specs, check_vma=False
    )
```

```python
import functools

import jax
import jax.numpy as jnp
from jax import lax
from jax.experimental import pallas as pl
from jax.experimental.pallas import tpu as pltpu
from jax.sharding import PartitionSpec as P

STEPS = 2
time_step = 0.2

FIELDS = 5
REACH = 9
HALO = REACH * STEPS
LANES = 256
STRIP = 32
PLANES = 4
SEGMENTS = 8

PAYLOAD = 464
SCALES = (-time_step / 60.0, -time_step * 45.0 / 60.0, -time_step)
KEEPS = (0.0, 0.0, 1.0)

f32 = jnp.float32
bf16 = jnp.bfloat16
f8 = jnp.float8_e5m2

HELD = 16.0


def iota(shape, axis):
    return lax.broadcasted_iota(jnp.int32, shape, axis)


def lane_index(shape, axis, rows):
    n = iota(shape, axis)
    own = rows * FIELDS
    h = n - own
    comp = jnp.where(n < own, n // rows, h // HALO)
    slot = jnp.where(n < own, HALO + n % rows, h % HALO)
    valid = n < own + FIELDS * HALO
    return jnp.where(valid, comp, -1), jnp.where(valid, slot, -100), n < own


def split(x):
    hi = x.astype(bf16)
    lo = (x - hi.astype(f32)).astype(bf16)
    return hi, lo


def split_small(x):
    hi = x.astype(bf16)
    return hi, (x - hi.astype(f32)).astype(f8)


def place(values, where_from):
    return jnp.dot(values.astype(bf16), where_from.astype(bf16), preferred_element_type=f32)


def head_or_tail(is_odd, block, first):
    rows = block.shape[0]
    tail, head = block[rows - HALO:], block[:HALO]
    return jnp.where(is_odd == first, head, tail)


def wall_strips(load, count):
    lane = iota((1, 128), 1)
    out = load(0)
    for q in range(1, count):
        out = jnp.where(lane >= q * STRIP, pltpu.roll(load(q), q * STRIP, axis=1), out)
    return out


def pack_mirror_kernel(
    rows, pert_hbm, ax_hbm, ae_hbm, sp_hbm, blow, mirror_out, pert, coefs, sems
):
    near = pl.ds(0, 128)
    copies = [
        pltpu.make_async_copy(pert_hbm.at[c, :, :, near], pert.at[c], sems.at[c])
        for c in range(FIELDS)
    ]
    for q, ref in enumerate((ax_hbm, ae_hbm, sp_hbm)):
        copies.append(
            pltpu.make_async_copy(ref.at[:, near], coefs.at[q], sems.at[FIELDS + q])
        )
    for copy in copies:
        copy.start()
    own = rows * FIELDS
    total = own + rows
    sub = iota((8, 128), 0)

    def reverse(block):
        groups = []
        for at in range(0, rows, 8):
            x = pltpu.roll(block[at:at + 8], 4, axis=0)
            for d in (2, 1):
                up, down = pltpu.roll(x, d, axis=0), pltpu.roll(x, 8 - d, axis=0)
                x = jnp.where((sub & d) != 0, up, down)
            groups.append(x)
        return jnp.concatenate(groups[::-1], axis=0)

    flags = jnp.broadcast_to(blow[...].astype(f32), (8, rows))
    a, b = iota((rows, 128), 0), iota((rows, 128), 1)
    mirror_out[total:total + 8] = place(flags, b == 2 * rows + rows - 1 - a)
    for copy in copies:
        copy.wait()
    for c in range(FIELDS):
        block = wall_strips(lambda k, c=c: pert[c, :, k, :], PLANES)
        mirror_out[c * rows:(c + 1) * rows] = reverse(block) * HELD
    mirror_out[own:total] = reverse(wall_strips(lambda q: coefs[q], 3))


def pack_strips_kernel(
    rows, me_ref, strips, even_in, odd_in, even_out, odd_out, stage, sems
):
    is_odd = me_ref[0] % 2
    own = rows * FIELDS
    b, a = iota((128, 128), 1), iota((128, 128), 0)
    copies = []
    for p, (out, first) in enumerate(((even_out, 1), (odd_out, 0))):
        parts = [
            head_or_tail(is_odd, strips[c * rows:(c + 1) * rows], first)
            for c in range(FIELDS)
        ]
        parts.append(jnp.zeros((6, 128), f32))
        parts.append(head_or_tail(is_odd, strips[own:own + rows], first))
        parts.append(jnp.zeros((24 - HALO, 128), f32))
        start = jnp.where(is_odd == first, 0, rows - HALO)
        base = own + 2 * HALO - 128
        parts.append(place(
            strips[own + rows:own + rows + 8],
            (b - base == a - 2 * rows - start) & (b >= base) & (b < base + HALO),
        ))
        block = jnp.concatenate(parts, axis=0)
        stage[p, :, 0:128] = block[0:64]
        stage[p, :, 128:256] = block[64:128]
        copy = pltpu.make_async_copy(
            stage.at[p], out.at[pl.ds(PAYLOAD, 64)], sems.at[p]
        )
        copy.start()
        copies.append(copy)
    for copy in copies:
        copy.wait()


def segments(block, hold, mid, store):
    hold[...] = block.T
    for js in range(SEGMENTS):
        for low in range(4):
            mid[low * 64 + js * 8:low * 64 + js * 8 + 8] = hold[
                pl.ds(js * 32 + low, 8, stride=4), :
            ]
    for low in range(4):
        for part in range(8):
            store(part * 4 + low, mid[pl.ds(low * 64 + part, SEGMENTS, stride=8), :])


def from_segments(load, hold, mid):
    for low in range(4):
        for part in range(8):
            mid[pl.ds(low * 64 + part, SEGMENTS, stride=8), :] = load(part * 4 + low)
    for js in range(SEGMENTS):
        for low in range(4):
            hold[pl.ds(js * 32 + low, 8, stride=4), :] = mid[
                low * 64 + js * 8:low * 64 + js * 8 + 8
            ]
    return hold[...].T


def prepare_kernel(
    rows, me_ref, cut_ref, cxi, ceta, cspan, pert_hbm, ax_hbm, ae_hbm, sp_hbm, blow,
    even_out, odd_out, xt, ct, last_field, wide, narrow, cuts,
    pert, coefs, hold, mid, sems,
):
    is_odd = me_ref[0] % 2
    copies = [pltpu.make_async_copy(pert_hbm, pert, sems.at[0])]
    for q, ref in enumerate((ax_hbm, ae_hbm, sp_hbm)):
        copies.append(pltpu.make_async_copy(ref, coefs.at[q], sems.at[1 + q]))
    for copy in copies:
        copy.start()
    own = rows * FIELDS
    cuts[...] = jnp.where(iota((8, 128), 0) == 0, cut_ref[0], cut_ref[1])
    slots = rows + HALO
    rc, rs, _ = lane_index((LANES, LANES), 0, rows)
    cc, cs, _ = lane_index((LANES, LANES), 1, rows)
    apart = jnp.where((rs >= 0) & (cs >= 0), (rs - cs + slots) % slots, 0)
    band = jnp.zeros((LANES, LANES), f32)
    for d, value in ((1, 45.0), (2, -9.0), (3, 1.0)):
        band = jnp.where(apart == d, value, band)
        band = jnp.where(apart == slots - d, -value, band)
    same = ((rs == cs) & (rs >= 0)).astype(f32)
    col_comp, _, _ = lane_index((1, LANES), 1, rows)

    def spread(matrix):
        total = jnp.zeros((LANES, LANES), f32)
        for d in range(FIELDS):
            line = jnp.zeros((1, LANES), f32)
            for c in range(FIELDS):
                line = jnp.where(col_comp == c, matrix[c, d], line)
            total = jnp.where(rc == d, line, total)
        return total

    xi = spread(cxi) * band * (-time_step / 60.0)
    eta = spread(ceta) * same * (-time_step * 45.0 / 60.0)
    span = spread(cspan) * same * (-time_step * 0.5)
    grad = jnp.where(rc == cc, band, 0.0)
    for w, first, small in ((xi, 0, 0), (eta, 2, 1), (grad, 4, 2), (span, 5, 3)):
        hi, lo = split(w)
        wide[first * LANES:(first + 1) * LANES] = hi
        if first != 4:
            wide[(first + 1) * LANES:(first + 2) * LANES] = lo
        narrow[small * LANES:(small + 1) * LANES] = w.astype(f8)
    for copy in copies:
        copy.wait()
    a, b = iota((rows, LANES), 0), iota((rows, LANES), 1)
    flags = jnp.broadcast_to(blow[...].astype(f32), (8, rows))
    for out, first in ((even_out, 1), (odd_out, 0)):
        for k in range(PLANES):
            for c in range(FIELDS):
                out[k * 96 + c * HALO:k * 96 + (c + 1) * HALO] = head_or_tail(
                    is_odd, pert[c, :, k, :], first
                ) * HELD
            out[k * 96 + 90:k * 96 + 96] = jnp.zeros((6, LANES), f32)
        for q in range(3):
            out[384 + q * 24:384 + q * 24 + HALO] = head_or_tail(is_odd, coefs[q], first)
            out[384 + q * 24 + HALO:384 + q * 24 + 24] = jnp.zeros((24 - HALO, LANES), f32)
        start = jnp.where(is_odd == first, 0, rows - HALO)
        base = own + 2 * HALO
        out[456:464] = place(flags, (b - base == a - start) & (b >= base) & (b < base + HALO))
        out[PAYLOAD:PAYLOAD + 64] = jnp.zeros((64, LANES), f32)
    for k in range(PLANES):
        block = HELD * jnp.concatenate([pert[c, :, k, :] for c in range(FIELDS - 1)], axis=0)

        def store(jl, slab, k=k):
            xt[k, jl] = slab

        segments(block, hold.at[k], mid.at[k], store)
        last_field[k] = pert[FIELDS - 1, :, k, :] * HELD
    for q in range(3):
        block = jnp.concatenate([coefs[q] * SCALES[q] + KEEPS[q]] * (FIELDS - 1), axis=0)

        def store(jl, slab, q=q):
            ct[q, jl] = slab

        segments(block, hold.at[PLANES + q], mid.at[PLANES + q], store)


def window_kernel(
    rows, total_rows, second, me_ref, blow, strips, xt, ct, last_field,
    wide, narrow, cuts, halo_in, *rest,
):
    if second:
        xe, ge, ce, gce, le = rest[:5]
        out, rest = rest[5], rest[6:]
    else:
        xe, ge, ce, gce, le = rest[:5]
        rest = rest[5:]
    (
        xs, v0, gs, gv, zz, partial, high, low, span_high, span_low,
        coef, gcoef, lanes_ref, wx, wx8, hold, mid, ghold,
    ) = rest
    me = me_ref[0]
    is_odd = me % 2
    own = rows * FIELDS
    slots = rows + HALO
    rs = lane_index((LANES, LANES), 0, rows)[1]

    def set_xi_weights(low, high):
        keep = jnp.where((rs >= low) & (rs < high), 0.0, 1.0)
        for source, kept, masked in ((wide, wx, (0, 1, 4)), (narrow, wx8, (0, 2))):
            for t in masked:
                block = source[t * LANES:(t + 1) * LANES]
                kept[t * LANES:(t + 1) * LANES] = (block.astype(f32) * keep).astype(block.dtype)

    def dot(a, w):
        return jnp.dot(a, w, preferred_element_type=f32)

    def twice(a):
        return jnp.concatenate([a, a], axis=1)

    def couple_ij(xh, eh, low):
        n = LANES
        first = dot(jnp.concatenate([xh, xh, eh, eh], axis=1), wx[0:4 * n])
        first8 = dot(low, wx8[0:2 * n])
        grad = dot(xh, wx[4 * n:5 * n])
        grad8 = dot(low[:, 0:n], wx8[2 * n:3 * n])
        return first, first8, grad, grad8

    def couple_k(sh, sl):
        n = LANES
        return dot(twice(sh), wx[5 * n:7 * n]) + dot(sl, wx8[3 * n:4 * n])

    comp, slot, is_own = lane_index((1, LANES), 1, rows)
    sign = jnp.where(comp == 2, -1.0, 1.0).astype(f32)
    a, b = iota((rows, LANES), 0), iota((rows, LANES), 1)
    own_flags = place(
        jnp.broadcast_to(blow[...].astype(f32), (8, rows)), b == 2 * rows + a
    )
    own_mirror = jnp.concatenate(
        [strips[own + rows:own + rows + 8], jnp.zeros((8, LANES - 128), f32)], axis=1
    )

    def cut_lanes(g):
        i = me * rows + g - HALO
        mirror = total_rows - 1 - i
        low, high = cuts[0:1, 0:1], cuts[1:2, 0:1]
        inside = ((i >= low) & (i < high)) | ((mirror >= low) & (mirror < high))
        return inside.astype(f32)

    def read_window(halo, halo_right):
        for k in range(PLANES):
            xs[k, 3:35, :, 0:128] = xt[k]
            v0[k, :, :, 0:128] = xt[k]

            def store(jl, slab, k=k):
                xs[k, 3 + jl, :, 128:256] = slab
                v0[k, jl, :, 128:256] = slab

            segments(
                jnp.concatenate([last_field[k], halo[k * 96:(k + 1) * 96]], axis=0),
                hold.at[k], mid.at[k], store,
            )
        for q in range(3):
            coef[q, :, :, 0:128] = ct[q]
            edge = halo[384 + q * 24:384 + q * 24 + HALO] * SCALES[q] + KEEPS[q]
            block = jnp.concatenate(
                [jnp.zeros((rows, LANES), f32)] + [edge] * FIELDS
                + [jnp.zeros((128 - rows - FIELDS * HALO, LANES), f32)], axis=0,
            )
            lane = iota((1, 128), 1)

            def store(jl, slab, q=q):
                coef[q, jl, :, 128:256] = jnp.where(lane < rows, ct[q, jl], slab)

            segments(block, hold.at[PLANES + q], mid.at[PLANES + q], store)
        near, far = halo[PAYLOAD:PAYLOAD + 64, 0:128], halo[PAYLOAD:PAYLOAD + 64, 128:256]
        last = strips[(FIELDS - 1) * rows:own]
        left = strips[0:128].T
        right = jnp.concatenate([last, near, far[0:32]], axis=0).T
        ghold[0, 0:128], ghold[0, 128:256] = left, right
        for m in range(HALO):
            for t in range(2):
                line = ghold[0, pl.ds(t * 128 + m, PLANES, stride=STRIP), :]
                gs[3 + m, 0:4, t * 128:(t + 1) * 128] = line
                gs[3 + m, 4:8, t * 128:(t + 1) * 128] = line
                gv[m, 0:4, t * 128:(t + 1) * 128] = line
                gv[m, 4:8, t * 128:(t + 1) * 128] = line
        mine, edge = strips[own:own + rows], far[32:32 + HALO]
        ghold[1, 0:128] = jnp.concatenate([mine] * (FIELDS - 1), axis=0).T
        ghold[1, 128:256] = jnp.concatenate(
            [mine] + [edge] * FIELDS
            + [jnp.zeros((128 - rows - FIELDS * HALO, 128), f32)], axis=0,
        ).T
        for q in range(3):
            for m in range(HALO):
                for t in range(2):
                    at = t * 128 + q * STRIP + m
                    gcoef[q, m, :, t * 128:(t + 1) * 128] = jnp.broadcast_to(
                        ghold[1, at:at + 1, :] * SCALES[q] + KEEPS[q], (8, 128)
                    )
        g = jnp.where(is_own, slot, jnp.where(halo_right == 1, slots + slot, slot))
        lanes_ref[0] = jnp.broadcast_to(cut_lanes(g), (8, LANES))
        lanes_ref[1] = 2.0 * (own_flags + halo[456:464])
        lanes_ref[2] = 2.0 * (
            own_mirror + jnp.concatenate([jnp.zeros((8, 128), f32), far[56:64]], axis=1)
        )

    sub = iota((8, LANES), 0)

    def pressure(line):
        near = pltpu.roll(line, LANES - 2 * rows, axis=1)
        far = pltpu.roll(line, LANES - 2 * HALO, axis=1)
        return jnp.where(is_own, near, far)

    def slopes(load, offset):
        return (
            (load(offset + 1) - load(offset - 1))
            - 0.2 * (load(offset + 2) - load(offset - 2))
            + (1.0 / 45.0) * (load(offset + 3) - load(offset - 3))
        )

    def time_stage(depth, alpha, beta):
        cut = lanes_ref[0] > 0.5
        wall = []
        for m in range(3):
            line = jnp.concatenate([xs[k, 3 + m, 0:1, :] for k in range(PLANES)], axis=0)
            wall.append(jnp.concatenate([line, line], axis=0))
        wall_g = [gs[3 + m] for m in range(3)]
        lift = lanes_ref[1] * jnp.where(comp == 2, pressure(wall[0]), 0.0)
        lift_g = lanes_ref[2] * jnp.where(comp == 2, pressure(wall_g[0]), 0.0)
        for m in range(3):
            ghost = jnp.where(cut, sign * wall_g[m], sign * wall[m] + lift)
            gs[2 - m] = jnp.where(cut, sign * wall[m], sign * wall_g[m] + lift_g)
            for k in range(PLANES):
                below = pltpu.roll(xs[k, 34 - m], 1, axis=0)
                xs[k, 2 - m] = jnp.where(sub == 0, ghost[k:k + 1], below)
                above = pltpu.roll(xs[k, 3 + m], SEGMENTS - 1, axis=0)
                xs[k, 35 + m] = jnp.where(sub == SEGMENTS - 1, 0.0, above)
        rows8 = 8 * SEGMENTS
        chunks = [(8 * c, slice(rows8 * c, rows8 * (c + 1))) for c in range(4)]

        def flat(v):
            return v.reshape(rows8, LANES)

        def split_plane(k):
            for at, here in chunks:
                x = flat(xs[k, 3 + at:11 + at])
                e = flat(slopes(lambda o: xs[k, at + o:at + o + 8], 3))
                cb, cd = flat(coef[1, at:at + 8]), flat(coef[2, at:at + 8])
                partial[k, here] = cb * e + cd * x
                xh, xl = split_small(x)
                eh, el = split_small(e)
                high[k, here, 0:LANES] = xh
                high[k, here, LANES:2 * LANES] = eh
                low[k, here, 0:LANES] = xl
                low[k, here, LANES:2 * LANES] = el

        for p in range(2):
            for at, here in chunks:
                s = xs[p + 1, 3 + at:11 + at] - xs[(p + 3) % PLANES, 3 + at:11 + at]
                span_high[p, here], span_low[p, here] = split_small(flat(s))
        split_plane(0)
        for p in range(2):
            zz[p] = couple_k(span_high[p], span_low[p])
        for k in range(PLANES):
            first, first8, grad, grad8 = couple_ij(
                high[k, :, 0:LANES], high[k, :, LANES:2 * LANES], low[k]
            )
            if k + 1 < PLANES:
                split_plane(k + 1)
            for at, here in chunks:
                ca = flat(coef[0, at:at + 8])
                r = (first[here] + first8[here]) + ca * (grad[here] + grad8[here])
                r = r + partial[k, here]
                r = r + zz[k, here] if k < 2 else r - zz[k - 2, here]
                r = alpha * flat(v0[k, at:at + 8]) + beta * r
                xs[k, 3 + at:11 + at] = r.reshape(8, SEGMENTS, LANES)
        n = depth * 8
        x = gs[3:3 + depth].reshape(n, LANES)
        e = slopes(lambda at: gs[at:at + depth], 3).reshape(n, LANES)
        xh, xl = split_small(x)
        eh, el = split_small(-e)
        first, first8, grad, grad8 = couple_ij(xh, eh, jnp.concatenate([xl, el], axis=1))
        s = gs[3:3 + depth]
        s = pltpu.roll(s, 7, axis=1) - pltpu.roll(s, 1, axis=1)
        z = couple_k(*split_small(s.reshape(n, LANES)))
        ca, cb, cd = (gcoef[q, 0:depth].reshape(n, LANES) for q in range(3))
        r = cb * e + cd * x - (first + first8) - ca * (grad + grad8) + z
        gs[3:3 + depth] = alpha * gv[0:depth] + beta * r.reshape(depth, 8, LANES)

    def time_steps(depth):
        def stage(s, carry):
            alpha = jnp.where(s == 0, 0.0, jnp.where(s == 1, 0.75, 1.0 / 3.0)).astype(f32)
            beta = jnp.where(s == 0, 1.0, jnp.where(s == 1, 0.25, 2.0 / 3.0)).astype(f32)
            time_stage(depth, alpha, beta)
            return carry

        lax.fori_loop(0, 3, stage, 0)

    at_start = me == 0
    at_end = me == total_rows // rows - 1
    gs[...] = jnp.zeros(gs.shape, f32)
    if not second:
        wx[...] = wide[...]
        wx8[...] = narrow[...]
        read_window(halo_in, 1 - is_odd)
        time_steps(HALO - 2)
        for k in range(PLANES):
            xe[k] = xs[k, 3:35]
        ge[...] = gs[3:3 + REACH]
        for q in range(3):
            ce[q] = coef[q, :, :, 128:256]
        gce[...] = gcoef[:, 0:REACH]
        le[...] = lanes_ref[...]
        return
    outside = at_start | at_end
    wx[...] = wide[...]
    wx8[...] = narrow[...]

    @pl.when(outside)
    def _():
        set_xi_weights(0, HALO)

    read_window(halo_in, is_odd)
    time_steps(HALO - 2)
    @pl.when(outside)
    def _():
        set_xi_weights(jnp.where(at_start, REACH, 0), jnp.where(at_start, HALO, REACH))

    left = (slot >= REACH) & (slot < REACH + rows)
    from_e = jnp.where(left, is_odd, 1 - is_odd) == 1
    for k in range(PLANES):
        merged = jnp.where(from_e, xe[k], xs[k, 3:35])
        xs[k, 3:35] = merged
        v0[k] = merged
    merged = jnp.where(from_e, ge[...], gs[3:3 + REACH])
    gs[3:3 + REACH] = merged
    gv[0:REACH] = merged
    coef[:, :, :, 128:256] = jnp.where(from_e[:, 128:256], ce[...], coef[:, :, :, 128:256])
    gcoef[:, 0:REACH] = jnp.where(from_e, gce[...], gcoef[:, 0:REACH])
    g = jnp.where(is_own, slot, jnp.where(slot < REACH, slots + slot, slot))
    lanes_ref[0] = jnp.broadcast_to(cut_lanes(g), (8, LANES))
    lanes_ref[1] = jnp.where(from_e, le[1], lanes_ref[1])
    lanes_ref[2] = jnp.where(from_e, le[2], lanes_ref[2])
    time_steps(REACH - 1)
    for k in range(PLANES):
        block = from_segments(
            lambda jl: xs[k, 3 + jl, :, 0:128], hold.at[k], mid.at[k]
        ) * (1.0 / HELD)
        for c in range(FIELDS - 1):
            out[c, :, k, :] = block[c * rows:(c + 1) * rows]
    lane = iota((1, 128), 1)

    def last_lanes(jl):
        line = xs[0, 3 + jl, :, 128:256]
        for k in range(1, PLANES):
            moved = pltpu.roll(xs[k, 3 + jl, :, 128:256], k * rows, axis=1)
            line = jnp.where(lane >= k * rows, moved, line)
        return line

    block = from_segments(last_lanes, hold.at[PLANES], mid.at[PLANES]) * (1.0 / HELD)
    for k in range(PLANES):
        out[FIELDS - 1, :, k, :] = block[k * rows:(k + 1) * rows]


def on_device(
    perturbation, advect_xi, advect_eta, sponge,
    couple_xi, couple_eta, couple_span, wake_cut, blowing,
):
    rows = perturbation.shape[1]
    devices = lax.axis_size("wrap")
    total_rows = rows * devices
    own = rows * FIELDS
    me = lax.axis_index("wrap").astype(jnp.int32).reshape(1)
    flags = blowing.reshape(1, rows)
    mirror = [(i, devices - 1 - i) for i in range(devices)]
    same_chip = [(i, i ^ 1) for i in range(devices)]
    next_chip = [(i, i + 1 if i % 2 else i - 1) for i in range(1, devices - 1)]

    vmem = pl.BlockSpec(memory_space=pltpu.VMEM)
    smem = pl.BlockSpec(memory_space=pltpu.SMEM)
    hbm = pl.BlockSpec(memory_space=pltpu.HBM)
    anywhere = pl.BlockSpec(memory_space=pl.ANY)

    def call(kernel, outs, ins, scratch, us, out_specs=None, vmem_kib=32 * 1024, **more):
        return pl.pallas_call(
            kernel,
            out_shape=outs,
            in_specs=ins,
            out_specs=out_specs or (vmem,) * len(outs),
            scratch_shapes=scratch,
            compiler_params=pltpu.CompilerParams(vmem_limit_bytes=vmem_kib * 1024),
            cost_estimate=pl.CostEstimate(
                flops=int(us * 1e9), bytes_accessed=int(us * 3e6), transcendentals=0
            ),
            **more,
        )

    def shape(*dims, dtype=f32):
        return jax.ShapeDtypeStruct(dims, dtype)

    dma = pltpu.SemaphoreType.DMA
    (to_mirror,) = call(
        functools.partial(pack_mirror_kernel, rows),
        (shape(own + rows + 8, 128),),
        [hbm] * 4 + [vmem],
        [
            pltpu.VMEM((FIELDS, rows, PLANES, 128), f32),
            pltpu.VMEM((3, rows, 128), f32),
            dma((FIELDS + 3,)),
        ],
        1,
        vmem_kib=64600,
    )(perturbation, advect_xi, advect_eta, sponge, flags)
    strips = lax.ppermute(to_mirror, "wrap", mirror)

    state = (PLANES, 32, SEGMENTS, LANES)
    payload = shape(PAYLOAD + 64, LANES)
    even, odd, xt, ct, last_field, wide, narrow, cuts = call(
        functools.partial(prepare_kernel, rows),
        (
            payload, payload,
            shape(PLANES, 32, SEGMENTS, 128), shape(3, 32, SEGMENTS, 128),
            shape(PLANES, rows, LANES),
            shape(7 * LANES, LANES, dtype=bf16), shape(4 * LANES, LANES, dtype=f8),
            shape(8, 128, dtype=jnp.int32),
        ),
        [smem] * 5 + [hbm] * 4 + [vmem],
        [
            pltpu.VMEM((FIELDS, rows, PLANES, LANES), f32),
            pltpu.VMEM((3, rows, LANES), f32),
            pltpu.VMEM((PLANES + 3, LANES, 128), f32),
            pltpu.VMEM((PLANES + 3, LANES, 128), f32),
            dma((4,)),
        ],
        4,
    )(
        me, wake_cut, couple_xi, couple_eta, couple_span,
        perturbation, advect_xi, advect_eta, sponge, flags,
    )
    even, odd = call(
        functools.partial(pack_strips_kernel, rows),
        (payload, payload),
        [smem, vmem, anywhere, anywhere],
        [pltpu.VMEM((2, 64, LANES), f32), dma((2,))],
        1,
        out_specs=(anywhere, anywhere),
        input_output_aliases={2: 0, 3: 1},
    )(me, strips, even, odd)
    from_next = lax.ppermute(odd, "wrap", next_chip)
    from_same = lax.ppermute(even, "wrap", same_chip)

    scratch = [
        pltpu.VMEM((PLANES, 38, SEGMENTS, LANES), f32),
        pltpu.VMEM(state, f32),
        pltpu.VMEM((3 + HALO + 3, 8, LANES), f32),
        pltpu.VMEM((HALO, 8, LANES), f32),
        pltpu.VMEM((2, LANES, LANES), f32),
        pltpu.VMEM((PLANES, LANES, LANES), f32),
        pltpu.VMEM((PLANES, LANES, 2 * LANES), bf16),
        pltpu.VMEM((PLANES, LANES, 2 * LANES), f8),
        pltpu.VMEM((2, LANES, LANES), bf16),
        pltpu.VMEM((2, LANES, LANES), f8),
        pltpu.VMEM((3, 32, SEGMENTS, LANES), f32),
        pltpu.VMEM((3, HALO, 8, LANES), f32),
        pltpu.VMEM((3, 8, LANES), f32),
        pltpu.VMEM((7 * LANES, LANES), bf16),
        pltpu.VMEM((4 * LANES, LANES), f8),
        pltpu.VMEM((PLANES + 3, LANES, 128), f32),
        pltpu.VMEM((PLANES + 3, LANES, 128), f32),
        pltpu.VMEM((2, LANES, 128), f32),
    ]
    common = (me, flags, strips, xt, ct, last_field, wide, narrow, cuts)
    specs = [smem] + [vmem] * 8
    first = call(
        functools.partial(window_kernel, rows, total_rows, False),
        (
            shape(*state), shape(REACH, 8, LANES), shape(3, 32, SEGMENTS, 128),
            shape(3, REACH, 8, LANES), shape(3, 8, LANES),
        ),
        specs + [vmem], scratch, 8,
    )(*common, from_same)
    (out,) = call(
        functools.partial(window_kernel, rows, total_rows, True),
        (shape(*perturbation.shape),),
        specs + [vmem] * 6, scratch, 14,
    )(*common, from_next, *first)
    return out


def solution(mesh):
    in_specs = (
        P(None, "wrap", None, None),
        P("wrap", None),
        P("wrap", None),
        P("wrap", None),
        P(),
        P(),
        P(),
        P(),
        P("wrap"),
    )
    out_specs = P(None, "wrap", None, None)
    return jax.shard_map(
        on_device, mesh=mesh, in_specs=in_specs, out_specs=out_specs, check_vma=False
    )
```

```python
import functools

import jax
import jax.numpy as jnp
from jax import lax
from jax.experimental import pallas as pl
from jax.experimental.pallas import tpu as pltpu
from jax.sharding import PartitionSpec as P

STEPS = 2
time_step = 0.2

FIELDS = 5
REACH = 9
HALO = REACH * STEPS
LANES = 256
STRIP = 32
PLANES = 4
SEGMENTS = 8

EDGE = 90
COEFS = 360
FLAGS = 416
PAYLOAD = 424
SCALES = (-time_step / 60.0, -time_step * 45.0 / 60.0, -time_step)
KEEPS = (0.0, 0.0, 1.0)

f32 = jnp.float32
bf16 = jnp.bfloat16
f8 = jnp.float8_e5m2

HELD = 16.0


def iota(shape, axis):
    return lax.broadcasted_iota(jnp.int32, shape, axis)


def lane_index(shape, axis, rows):
    n = iota(shape, axis)
    own = rows * FIELDS
    h = n - own
    comp = jnp.where(n < own, n // rows, h // HALO)
    slot = jnp.where(n < own, HALO + n % rows, h % HALO)
    valid = n < own + FIELDS * HALO
    return jnp.where(valid, comp, -1), jnp.where(valid, slot, -100), n < own


def split(x):
    hi = x.astype(bf16)
    lo = (x - hi.astype(f32)).astype(bf16)
    return hi, lo


def split_small(x):
    hi = x.astype(bf16)
    return hi, (x - hi.astype(f32)).astype(f8)


def place(values, where_from):
    return jnp.dot(values.astype(bf16), where_from.astype(bf16), preferred_element_type=f32)


def head_or_tail(is_odd, block, first):
    rows = block.shape[0]
    tail, head = block[rows - HALO:], block[:HALO]
    return jnp.where(is_odd == first, head, tail)


def wall_strips(load, count):
    lane = iota((1, 128), 1)
    out = load(0)
    for q in range(1, count):
        out = jnp.where(lane >= q * STRIP, pltpu.roll(load(q), q * STRIP, axis=1), out)
    return out


def pack_mirror_kernel(
    rows, pert_hbm, ax_hbm, ae_hbm, sp_hbm, blow, mirror_out, pert, coefs, sems
):
    near = pl.ds(0, 128)
    copies = [
        pltpu.make_async_copy(pert_hbm.at[c, :, :, near], pert.at[c], sems.at[c])
        for c in range(FIELDS)
    ]
    for q, ref in enumerate((ax_hbm, ae_hbm, sp_hbm)):
        copies.append(
            pltpu.make_async_copy(ref.at[:, near], coefs.at[q], sems.at[FIELDS + q])
        )
    for copy in copies:
        copy.start()
    own = rows * FIELDS
    total = own + rows
    sub = iota((8, 128), 0)

    def reverse(block):
        groups = []
        for at in range(0, rows, 8):
            x = pltpu.roll(block[at:at + 8], 4, axis=0)
            for d in (2, 1):
                up, down = pltpu.roll(x, d, axis=0), pltpu.roll(x, 8 - d, axis=0)
                x = jnp.where((sub & d) != 0, up, down)
            groups.append(x)
        return jnp.concatenate(groups[::-1], axis=0)

    flags = jnp.broadcast_to(blow[...].astype(f32), (8, rows))
    a, b = iota((rows, 128), 0), iota((rows, 128), 1)
    mirror_out[total:total + 8] = place(flags, b == 2 * rows + rows - 1 - a)
    for copy in copies:
        copy.wait()
    for c in range(FIELDS):
        block = wall_strips(lambda k, c=c: pert[c, :, k, :], PLANES)
        mirror_out[c * rows:(c + 1) * rows] = reverse(block) * HELD
    mirror_out[own:total] = reverse(wall_strips(lambda q: coefs[q], 3))


def pack_strips_kernel(
    rows, me_ref, strips, even_in, odd_in, even_out, odd_out, stage, sems
):
    is_odd = me_ref[0] % 2
    own = rows * FIELDS
    b, a = iota((128, 128), 1), iota((128, 128), 0)
    copies = []
    for p, (out, first) in enumerate(((even_out, 1), (odd_out, 0))):
        parts = [
            head_or_tail(is_odd, strips[c * rows:(c + 1) * rows], first)
            for c in range(FIELDS)
        ]
        parts.append(jnp.zeros((6, 128), f32))
        parts.append(head_or_tail(is_odd, strips[own:own + rows], first))
        parts.append(jnp.zeros((24 - HALO, 128), f32))
        start = jnp.where(is_odd == first, 0, rows - HALO)
        base = own + 2 * HALO - 128
        parts.append(place(
            strips[own + rows:own + rows + 8],
            (b - base == a - 2 * rows - start) & (b >= base) & (b < base + HALO),
        ))
        block = jnp.concatenate(parts, axis=0)
        stage[p, :, 0:128] = block[0:64]
        stage[p, :, 128:256] = block[64:128]
        copy = pltpu.make_async_copy(
            stage.at[p], out.at[pl.ds(PAYLOAD, 64)], sems.at[p]
        )
        copy.start()
        copies.append(copy)
    for copy in copies:
        copy.wait()


def segments(block, hold, mid, store):
    hold[...] = block.T
    for js in range(SEGMENTS):
        for low in range(4):
            mid[low * 64 + js * 8:low * 64 + js * 8 + 8] = hold[
                pl.ds(js * 32 + low, 8, stride=4), :
            ]
    for low in range(4):
        for part in range(8):
            store(part * 4 + low, mid[pl.ds(low * 64 + part, SEGMENTS, stride=8), :])


def from_segments(load, hold, mid):
    for low in range(4):
        for part in range(8):
            mid[pl.ds(low * 64 + part, SEGMENTS, stride=8), :] = load(part * 4 + low)
    for js in range(SEGMENTS):
        for low in range(4):
            hold[pl.ds(js * 32 + low, 8, stride=4), :] = mid[
                low * 64 + js * 8:low * 64 + js * 8 + 8
            ]
    return hold[...].T


def prepare_kernel(
    rows, me_ref, cut_ref, cxi, ceta, cspan, pert_hbm, ax_hbm, ae_hbm, sp_hbm, blow,
    even_out, odd_out, xt, ct, last_field, wide, narrow, cuts,
    pert, coefs, hold, mid, sems,
):
    is_odd = me_ref[0] % 2
    copies = [pltpu.make_async_copy(pert_hbm, pert, sems.at[0])]
    for q, ref in enumerate((ax_hbm, ae_hbm, sp_hbm)):
        copies.append(pltpu.make_async_copy(ref, coefs.at[q], sems.at[1 + q]))
    for copy in copies:
        copy.start()
    own = rows * FIELDS
    cuts[...] = jnp.where(iota((8, 128), 0) == 0, cut_ref[0], cut_ref[1])
    slots = rows + HALO
    rc, rs, _ = lane_index((LANES, LANES), 0, rows)
    cc, cs, _ = lane_index((LANES, LANES), 1, rows)
    apart = jnp.where((rs >= 0) & (cs >= 0), (rs - cs + slots) % slots, 0)
    band = jnp.zeros((LANES, LANES), f32)
    for d, value in ((1, 45.0), (2, -9.0), (3, 1.0)):
        band = jnp.where(apart == d, value, band)
        band = jnp.where(apart == slots - d, -value, band)
    same = ((rs == cs) & (rs >= 0)).astype(f32)
    col_comp, _, _ = lane_index((1, LANES), 1, rows)

    def spread(matrix):
        total = jnp.zeros((LANES, LANES), f32)
        for d in range(FIELDS):
            line = jnp.zeros((1, LANES), f32)
            for c in range(FIELDS):
                line = jnp.where(col_comp == c, matrix[c, d], line)
            total = jnp.where(rc == d, line, total)
        return total

    xi = spread(cxi) * band * (-time_step / 60.0)
    eta = spread(ceta) * same * (-time_step * 45.0 / 60.0)
    span = spread(cspan) * same * (-time_step * 0.5)
    grad = jnp.where(rc == cc, band, 0.0)
    for w, first, small in ((xi, 0, 0), (eta, 2, 1), (grad, 4, 2), (span, 5, 3)):
        hi, lo = split(w)
        wide[first * LANES:(first + 1) * LANES] = hi
        if first != 4:
            wide[(first + 1) * LANES:(first + 2) * LANES] = lo
        narrow[small * LANES:(small + 1) * LANES] = w.astype(f8)
    for copy in copies:
        copy.wait()
    a, b = iota((rows, LANES), 0), iota((rows, LANES), 1)
    flags = jnp.broadcast_to(blow[...].astype(f32), (8, rows))
    for out, first in ((even_out, 1), (odd_out, 0)):
        for k in range(PLANES):
            for c in range(FIELDS):
                out[k * EDGE + c * HALO:k * EDGE + (c + 1) * HALO] = head_or_tail(
                    is_odd, pert[c, :, k, :], first
                ) * HELD
        for q in range(3):
            out[COEFS + q * HALO:COEFS + (q + 1) * HALO] = head_or_tail(is_odd, coefs[q], first)
        out[COEFS + 3 * HALO:FLAGS] = jnp.zeros((FLAGS - COEFS - 3 * HALO, LANES), f32)
        start = jnp.where(is_odd == first, 0, rows - HALO)
        base = own + 2 * HALO
        out[FLAGS:PAYLOAD] = place(flags, (b - base == a - start) & (b >= base) & (b < base + HALO))
        out[PAYLOAD:PAYLOAD + 64] = jnp.zeros((64, LANES), f32)
    for k in range(PLANES):
        block = HELD * jnp.concatenate([pert[c, :, k, :] for c in range(FIELDS - 1)], axis=0)

        def store(jl, slab, k=k):
            xt[k, jl] = slab

        segments(block, hold.at[k], mid.at[k], store)
        last_field[k] = pert[FIELDS - 1, :, k, :] * HELD
    for q in range(3):
        block = jnp.concatenate([coefs[q] * SCALES[q] + KEEPS[q]] * (FIELDS - 1), axis=0)

        def store(jl, slab, q=q):
            ct[q, jl] = slab

        segments(block, hold.at[PLANES + q], mid.at[PLANES + q], store)


def window_kernel(
    rows, total_rows, second, me_ref, blow, strips, xt, ct, last_field,
    wide, narrow, cuts, halo_in, *rest,
):
    if second:
        xe, ge, ce, gce, le = rest[:5]
        out, rest = rest[5], rest[6:]
    else:
        xe, ge, ce, gce, le = rest[:5]
        rest = rest[5:]
    (
        xs, v0, gs, gv, zz, partial, high, low, span_high, span_low,
        coef, gcoef, lanes_ref, wx, wx8, hold, mid, ghold,
    ) = rest
    me = me_ref[0]
    is_odd = me % 2
    own = rows * FIELDS
    slots = rows + HALO
    rs = lane_index((LANES, LANES), 0, rows)[1]

    def set_xi_weights(low, high):
        keep = jnp.where((rs >= low) & (rs < high), 0.0, 1.0)
        for source, kept, masked in ((wide, wx, (0, 1, 4)), (narrow, wx8, (0, 2))):
            for t in masked:
                block = source[t * LANES:(t + 1) * LANES]
                kept[t * LANES:(t + 1) * LANES] = (block.astype(f32) * keep).astype(block.dtype)

    def dot(a, w):
        return jnp.dot(a, w, preferred_element_type=f32)

    def twice(a):
        return jnp.concatenate([a, a], axis=1)

    def couple_ij(xh, eh, low):
        n = LANES
        first = dot(jnp.concatenate([xh, xh, eh, eh], axis=1), wx[0:4 * n])
        first8 = dot(low, wx8[0:2 * n])
        grad = dot(xh, wx[4 * n:5 * n])
        grad8 = dot(low[:, 0:n], wx8[2 * n:3 * n])
        return first, first8, grad, grad8

    def couple_k(sh, sl):
        n = LANES
        return dot(twice(sh), wx[5 * n:7 * n]) + dot(sl, wx8[3 * n:4 * n])

    comp, slot, is_own = lane_index((1, LANES), 1, rows)
    sign = jnp.where(comp == 2, -1.0, 1.0).astype(f32)
    a, b = iota((rows, LANES), 0), iota((rows, LANES), 1)
    own_flags = place(
        jnp.broadcast_to(blow[...].astype(f32), (8, rows)), b == 2 * rows + a
    )
    own_mirror = jnp.concatenate(
        [strips[own + rows:own + rows + 8], jnp.zeros((8, LANES - 128), f32)], axis=1
    )

    def cut_lanes(g):
        i = me * rows + g - HALO
        mirror = total_rows - 1 - i
        low, high = cuts[0:1, 0:1], cuts[1:2, 0:1]
        inside = ((i >= low) & (i < high)) | ((mirror >= low) & (mirror < high))
        return inside.astype(f32)

    def read_window(halo, halo_right):
        for k in range(PLANES):
            xs[k, 3:35, :, 0:128] = xt[k]
            v0[k, :, :, 0:128] = xt[k]

            def store(jl, slab, k=k):
                xs[k, 3 + jl, :, 128:256] = slab
                v0[k, jl, :, 128:256] = slab

            segments(
                jnp.concatenate(
                    [last_field[k], halo[k * EDGE:(k + 1) * EDGE], jnp.zeros((6, LANES), f32)],
                    axis=0,
                ),
                hold.at[k], mid.at[k], store,
            )
        for q in range(3):
            coef[q, :, :, 0:128] = ct[q]
            edge = halo[COEFS + q * HALO:COEFS + (q + 1) * HALO] * SCALES[q] + KEEPS[q]
            block = jnp.concatenate(
                [jnp.zeros((rows, LANES), f32)] + [edge] * FIELDS
                + [jnp.zeros((128 - rows - FIELDS * HALO, LANES), f32)], axis=0,
            )
            lane = iota((1, 128), 1)

            def store(jl, slab, q=q):
                coef[q, jl, :, 128:256] = jnp.where(lane < rows, ct[q, jl], slab)

            segments(block, hold.at[PLANES + q], mid.at[PLANES + q], store)
        near, far = halo[PAYLOAD:PAYLOAD + 64, 0:128], halo[PAYLOAD:PAYLOAD + 64, 128:256]
        last = strips[(FIELDS - 1) * rows:own]
        left = strips[0:128].T
        right = jnp.concatenate([last, near, far[0:32]], axis=0).T
        ghold[0, 0:128], ghold[0, 128:256] = left, right
        for m in range(HALO):
            for t in range(2):
                line = ghold[0, pl.ds(t * 128 + m, PLANES, stride=STRIP), :]
                gs[3 + m, 0:4, t * 128:(t + 1) * 128] = line
                gs[3 + m, 4:8, t * 128:(t + 1) * 128] = line
                gv[m, 0:4, t * 128:(t + 1) * 128] = line
                gv[m, 4:8, t * 128:(t + 1) * 128] = line
        mine, edge = strips[own:own + rows], far[32:32 + HALO]
        ghold[1, 0:128] = jnp.concatenate([mine] * (FIELDS - 1), axis=0).T
        ghold[1, 128:256] = jnp.concatenate(
            [mine] + [edge] * FIELDS
            + [jnp.zeros((128 - rows - FIELDS * HALO, 128), f32)], axis=0,
        ).T
        for q in range(3):
            for m in range(HALO):
                for t in range(2):
                    at = t * 128 + q * STRIP + m
                    gcoef[q, m, :, t * 128:(t + 1) * 128] = jnp.broadcast_to(
                        ghold[1, at:at + 1, :] * SCALES[q] + KEEPS[q], (8, 128)
                    )
        g = jnp.where(is_own, slot, jnp.where(halo_right == 1, slots + slot, slot))
        lanes_ref[0] = jnp.broadcast_to(cut_lanes(g), (8, LANES))
        lanes_ref[1] = 2.0 * (own_flags + halo[FLAGS:PAYLOAD])
        lanes_ref[2] = 2.0 * (
            own_mirror + jnp.concatenate([jnp.zeros((8, 128), f32), far[56:64]], axis=1)
        )

    sub = iota((8, LANES), 0)

    def pressure(line):
        near = pltpu.roll(line, LANES - 2 * rows, axis=1)
        far = pltpu.roll(line, LANES - 2 * HALO, axis=1)
        return jnp.where(is_own, near, far)

    def slopes(load, offset):
        return (
            (load(offset + 1) - load(offset - 1))
            - 0.2 * (load(offset + 2) - load(offset - 2))
            + (1.0 / 45.0) * (load(offset + 3) - load(offset - 3))
        )

    def time_stage(depth, alpha, beta):
        cut = lanes_ref[0] > 0.5
        wall = []
        for m in range(3):
            line = jnp.concatenate([xs[k, 3 + m, 0:1, :] for k in range(PLANES)], axis=0)
            wall.append(jnp.concatenate([line, line], axis=0))
        wall_g = [gs[3 + m] for m in range(3)]
        lift = lanes_ref[1] * jnp.where(comp == 2, pressure(wall[0]), 0.0)
        lift_g = lanes_ref[2] * jnp.where(comp == 2, pressure(wall_g[0]), 0.0)
        for m in range(3):
            ghost = jnp.where(cut, sign * wall_g[m], sign * wall[m] + lift)
            gs[2 - m] = jnp.where(cut, sign * wall[m], sign * wall_g[m] + lift_g)
            for k in range(PLANES):
                below = pltpu.roll(xs[k, 34 - m], 1, axis=0)
                xs[k, 2 - m] = jnp.where(sub == 0, ghost[k:k + 1], below)
                above = pltpu.roll(xs[k, 3 + m], SEGMENTS - 1, axis=0)
                xs[k, 35 + m] = jnp.where(sub == SEGMENTS - 1, 0.0, above)
        rows8 = 8 * SEGMENTS
        chunks = [(8 * c, slice(rows8 * c, rows8 * (c + 1))) for c in range(4)]

        def flat(v):
            return v.reshape(rows8, LANES)

        def split_plane(k):
            for at, here in chunks:
                x = flat(xs[k, 3 + at:11 + at])
                e = flat(slopes(lambda o: xs[k, at + o:at + o + 8], 3))
                cb, cd = flat(coef[1, at:at + 8]), flat(coef[2, at:at + 8])
                partial[k, here] = cb * e + cd * x
                xh, xl = split_small(x)
                eh, el = split_small(e)
                high[k, here, 0:LANES] = xh
                high[k, here, LANES:2 * LANES] = eh
                low[k, here, 0:LANES] = xl
                low[k, here, LANES:2 * LANES] = el

        for p in range(2):
            for at, here in chunks:
                s = xs[p + 1, 3 + at:11 + at] - xs[(p + 3) % PLANES, 3 + at:11 + at]
                span_high[p, here], span_low[p, here] = split_small(flat(s))
        split_plane(0)
        for p in range(2):
            zz[p] = couple_k(span_high[p], span_low[p])
        for k in range(PLANES):
            first, first8, grad, grad8 = couple_ij(
                high[k, :, 0:LANES], high[k, :, LANES:2 * LANES], low[k]
            )
            if k + 1 < PLANES:
                split_plane(k + 1)
            for at, here in chunks:
                ca = flat(coef[0, at:at + 8])
                r = (first[here] + first8[here]) + ca * (grad[here] + grad8[here])
                r = r + partial[k, here]
                r = r + zz[k, here] if k < 2 else r - zz[k - 2, here]
                if not isinstance(alpha, float) or alpha:
                    r = alpha * flat(v0[k, at:at + 8]) + beta * r
                xs[k, 3 + at:11 + at] = r.reshape(8, SEGMENTS, LANES)
        n = depth * 8
        x = gs[3:3 + depth].reshape(n, LANES)
        e = slopes(lambda at: gs[at:at + depth], 3).reshape(n, LANES)
        xh, xl = split_small(x)
        eh, el = split_small(-e)
        first, first8, grad, grad8 = couple_ij(xh, eh, jnp.concatenate([xl, el], axis=1))
        s = gs[3:3 + depth]
        s = pltpu.roll(s, 7, axis=1) - pltpu.roll(s, 1, axis=1)
        z = couple_k(*split_small(s.reshape(n, LANES)))
        ca, cb, cd = (gcoef[q, 0:depth].reshape(n, LANES) for q in range(3))
        r = cb * e + cd * x - (first + first8) - ca * (grad + grad8) + z
        r = r.reshape(depth, 8, LANES)
        if not isinstance(alpha, float) or alpha:
            r = alpha * gv[0:depth] + beta * r
        gs[3:3 + depth] = r

    def time_steps(depth):
        weights = ((0.0, 1.0), (0.75, 0.25), (1.0 / 3.0, 2.0 / 3.0))
        if second:
            for alpha, beta in weights:
                time_stage(depth, alpha, beta)
            return

        def stage(s, carry):
            alpha, beta = (
                jnp.where(s == 0, w[0], jnp.where(s == 1, w[1], w[2])).astype(f32)
                for w in zip(*weights)
            )
            time_stage(depth, alpha, beta)
            return carry

        lax.fori_loop(0, 3, stage, 0)

    at_start = me == 0
    at_end = me == total_rows // rows - 1
    gs[...] = jnp.zeros(gs.shape, f32)
    if not second:
        wx[...] = wide[...]
        wx8[...] = narrow[...]
        read_window(halo_in, 1 - is_odd)
        time_steps(HALO - 2)
        for k in range(PLANES):
            xe[k] = xs[k, 3:35]
        ge[...] = gs[3:3 + REACH]
        for q in range(3):
            ce[q] = coef[q, :, :, 128:256]
        gce[...] = gcoef[:, 0:REACH]
        le[...] = lanes_ref[...]
        return
    outside = at_start | at_end
    wx[...] = wide[...]
    wx8[...] = narrow[...]

    @pl.when(outside)
    def _():
        set_xi_weights(0, HALO)

    read_window(halo_in, is_odd)
    time_steps(HALO - 2)
    @pl.when(outside)
    def _():
        set_xi_weights(jnp.where(at_start, REACH, 0), jnp.where(at_start, HALO, REACH))

    left = (slot >= REACH) & (slot < REACH + rows)
    from_e = jnp.where(left, is_odd, 1 - is_odd) == 1
    for k in range(PLANES):
        merged = jnp.where(from_e, xe[k], xs[k, 3:35])
        xs[k, 3:35] = merged
        v0[k] = merged
    merged = jnp.where(from_e, ge[...], gs[3:3 + REACH])
    gs[3:3 + REACH] = merged
    gv[0:REACH] = merged
    coef[:, :, :, 128:256] = jnp.where(from_e[:, 128:256], ce[...], coef[:, :, :, 128:256])
    gcoef[:, 0:REACH] = jnp.where(from_e, gce[...], gcoef[:, 0:REACH])
    g = jnp.where(is_own, slot, jnp.where(slot < REACH, slots + slot, slot))
    lanes_ref[0] = jnp.broadcast_to(cut_lanes(g), (8, LANES))
    lanes_ref[1] = jnp.where(from_e, le[1], lanes_ref[1])
    lanes_ref[2] = jnp.where(from_e, le[2], lanes_ref[2])
    time_steps(REACH - 1)
    for k in range(PLANES):
        block = from_segments(
            lambda jl: xs[k, 3 + jl, :, 0:128], hold.at[k], mid.at[k]
        ) * (1.0 / HELD)
        for c in range(FIELDS - 1):
            out[c, :, k, :] = block[c * rows:(c + 1) * rows]
    lane = iota((1, 128), 1)

    def last_lanes(jl):
        line = xs[0, 3 + jl, :, 128:256]
        for k in range(1, PLANES):
            moved = pltpu.roll(xs[k, 3 + jl, :, 128:256], k * rows, axis=1)
            line = jnp.where(lane >= k * rows, moved, line)
        return line

    block = from_segments(last_lanes, hold.at[PLANES], mid.at[PLANES]) * (1.0 / HELD)
    for k in range(PLANES):
        out[FIELDS - 1, :, k, :] = block[k * rows:(k + 1) * rows]


def on_device(
    perturbation, advect_xi, advect_eta, sponge,
    couple_xi, couple_eta, couple_span, wake_cut, blowing,
):
    rows = perturbation.shape[1]
    devices = lax.axis_size("wrap")
    total_rows = rows * devices
    own = rows * FIELDS
    me = lax.axis_index("wrap").astype(jnp.int32).reshape(1)
    flags = blowing.reshape(1, rows)
    mirror = [(i, devices - 1 - i) for i in range(devices)]
    same_chip = [(i, i ^ 1) for i in range(devices)]
    next_chip = [(i, i + 1 if i % 2 else i - 1) for i in range(1, devices - 1)]

    vmem = pl.BlockSpec(memory_space=pltpu.VMEM)
    smem = pl.BlockSpec(memory_space=pltpu.SMEM)
    hbm = pl.BlockSpec(memory_space=pltpu.HBM)
    anywhere = pl.BlockSpec(memory_space=pl.ANY)

    def call(kernel, outs, ins, scratch, us, out_specs=None, vmem_kib=32 * 1024, **more):
        return pl.pallas_call(
            kernel,
            out_shape=outs,
            in_specs=ins,
            out_specs=out_specs or (vmem,) * len(outs),
            scratch_shapes=scratch,
            compiler_params=pltpu.CompilerParams(vmem_limit_bytes=vmem_kib * 1024),
            cost_estimate=pl.CostEstimate(
                flops=int(us * 1e9), bytes_accessed=int(us * 3e6), transcendentals=0
            ),
            **more,
        )

    def shape(*dims, dtype=f32):
        return jax.ShapeDtypeStruct(dims, dtype)

    dma = pltpu.SemaphoreType.DMA
    (to_mirror,) = call(
        functools.partial(pack_mirror_kernel, rows),
        (shape(own + rows + 8, 128),),
        [hbm] * 4 + [vmem],
        [
            pltpu.VMEM((FIELDS, rows, PLANES, 128), f32),
            pltpu.VMEM((3, rows, 128), f32),
            dma((FIELDS + 3,)),
        ],
        1,
        vmem_kib=64600,
    )(perturbation, advect_xi, advect_eta, sponge, flags)
    strips = lax.ppermute(to_mirror, "wrap", mirror)

    state = (PLANES, 32, SEGMENTS, LANES)
    payload = shape(PAYLOAD + 64, LANES)
    even, odd, xt, ct, last_field, wide, narrow, cuts = call(
        functools.partial(prepare_kernel, rows),
        (
            payload, payload,
            shape(PLANES, 32, SEGMENTS, 128), shape(3, 32, SEGMENTS, 128),
            shape(PLANES, rows, LANES),
            shape(7 * LANES, LANES, dtype=bf16), shape(4 * LANES, LANES, dtype=f8),
            shape(8, 128, dtype=jnp.int32),
        ),
        [smem] * 5 + [hbm] * 4 + [vmem],
        [
            pltpu.VMEM((FIELDS, rows, PLANES, LANES), f32),
            pltpu.VMEM((3, rows, LANES), f32),
            pltpu.VMEM((PLANES + 3, LANES, 128), f32),
            pltpu.VMEM((PLANES + 3, LANES, 128), f32),
            dma((4,)),
        ],
        4,
    )(
        me, wake_cut, couple_xi, couple_eta, couple_span,
        perturbation, advect_xi, advect_eta, sponge, flags,
    )
    even, odd = call(
        functools.partial(pack_strips_kernel, rows),
        (payload, payload),
        [smem, vmem, anywhere, anywhere],
        [pltpu.VMEM((2, 64, LANES), f32), dma((2,))],
        1,
        out_specs=(anywhere, anywhere),
        input_output_aliases={2: 0, 3: 1},
    )(me, strips, even, odd)
    from_next = lax.ppermute(odd, "wrap", next_chip)
    from_same = lax.ppermute(even, "wrap", same_chip)

    scratch = [
        pltpu.VMEM((PLANES, 38, SEGMENTS, LANES), f32),
        pltpu.VMEM(state, f32),
        pltpu.VMEM((3 + HALO + 3, 8, LANES), f32),
        pltpu.VMEM((HALO, 8, LANES), f32),
        pltpu.VMEM((2, LANES, LANES), f32),
        pltpu.VMEM((PLANES, LANES, LANES), f32),
        pltpu.VMEM((PLANES, LANES, 2 * LANES), bf16),
        pltpu.VMEM((PLANES, LANES, 2 * LANES), f8),
        pltpu.VMEM((2, LANES, LANES), bf16),
        pltpu.VMEM((2, LANES, LANES), f8),
        pltpu.VMEM((3, 32, SEGMENTS, LANES), f32),
        pltpu.VMEM((3, HALO, 8, LANES), f32),
        pltpu.VMEM((3, 8, LANES), f32),
        pltpu.VMEM((7 * LANES, LANES), bf16),
        pltpu.VMEM((4 * LANES, LANES), f8),
        pltpu.VMEM((PLANES + 3, LANES, 128), f32),
        pltpu.VMEM((PLANES + 3, LANES, 128), f32),
        pltpu.VMEM((2, LANES, 128), f32),
    ]
    common = (me, flags, strips, xt, ct, last_field, wide, narrow, cuts)
    specs = [smem] + [vmem] * 8
    first = call(
        functools.partial(window_kernel, rows, total_rows, False),
        (
            shape(*state), shape(REACH, 8, LANES), shape(3, 32, SEGMENTS, 128),
            shape(3, REACH, 8, LANES), shape(3, 8, LANES),
        ),
        specs + [vmem], scratch, 8,
    )(*common, from_same)
    (out,) = call(
        functools.partial(window_kernel, rows, total_rows, True),
        (shape(*perturbation.shape),),
        specs + [vmem] * 6, scratch, 14,
    )(*common, from_next, *first)
    return out


def solution(mesh):
    in_specs = (
        P(None, "wrap", None, None),
        P("wrap", None),
        P("wrap", None),
        P("wrap", None),
        P(),
        P(),
        P(),
        P(),
        P("wrap"),
    )
    out_specs = P(None, "wrap", None, None)
    return jax.shard_map(
        on_device, mesh=mesh, in_specs=in_specs, out_specs=out_specs, check_vma=False
    )
```

```python
import functools

import jax
import jax.numpy as jnp
from jax import lax
from jax.experimental import pallas as pl
from jax.experimental.pallas import tpu as pltpu
from jax.sharding import PartitionSpec as P

STEPS = 2
time_step = 0.2

FIELDS = 5
REACH = 9
HALO = REACH * STEPS
LANES = 256
STRIP = 32
PLANES = 4
SEGMENTS = 8

EDGE = 90
COEFS = 360
FLAGS = 416
PAYLOAD = 424
SCALES = (-time_step / 60.0, -time_step * 45.0 / 60.0, -time_step)
KEEPS = (0.0, 0.0, 1.0)

f32 = jnp.float32
bf16 = jnp.bfloat16
f8 = jnp.float8_e5m2

HELD = 16.0


def iota(shape, axis):
    return lax.broadcasted_iota(jnp.int32, shape, axis)


def lane_index(shape, axis, rows):
    n = iota(shape, axis)
    own = rows * FIELDS
    h = n - own
    comp = jnp.where(n < own, n // rows, h // HALO)
    slot = jnp.where(n < own, HALO + n % rows, h % HALO)
    valid = n < own + FIELDS * HALO
    return jnp.where(valid, comp, -1), jnp.where(valid, slot, -100), n < own


def split(x):
    hi = x.astype(bf16)
    lo = (x - hi.astype(f32)).astype(bf16)
    return hi, lo


def split_small(x):
    hi = x.astype(bf16)
    return hi, (x - hi.astype(f32)).astype(f8)


def place(values, where_from):
    return jnp.dot(values.astype(bf16), where_from.astype(bf16), preferred_element_type=f32)


def head_or_tail(is_odd, block, first):
    rows = block.shape[0]
    tail, head = block[rows - HALO:], block[:HALO]
    return jnp.where(is_odd == first, head, tail)


def wall_strips(load, count):
    lane = iota((1, 128), 1)
    out = load(0)
    for q in range(1, count):
        out = jnp.where(lane >= q * STRIP, pltpu.roll(load(q), q * STRIP, axis=1), out)
    return out


def pack_mirror_kernel(
    rows, pert_hbm, ax_hbm, ae_hbm, sp_hbm, blow, mirror_out, pert, coefs, sems
):
    near = pl.ds(0, 128)
    copies = [
        pltpu.make_async_copy(pert_hbm.at[c, :, :, near], pert.at[c], sems.at[c])
        for c in range(FIELDS)
    ]
    for q, ref in enumerate((ax_hbm, ae_hbm, sp_hbm)):
        copies.append(
            pltpu.make_async_copy(ref.at[:, near], coefs.at[q], sems.at[FIELDS + q])
        )
    for copy in copies:
        copy.start()
    own = rows * FIELDS
    total = own + rows
    sub = iota((8, 128), 0)

    def reverse(block):
        groups = []
        for at in range(0, rows, 8):
            x = pltpu.roll(block[at:at + 8], 4, axis=0)
            for d in (2, 1):
                up, down = pltpu.roll(x, d, axis=0), pltpu.roll(x, 8 - d, axis=0)
                x = jnp.where((sub & d) != 0, up, down)
            groups.append(x)
        return jnp.concatenate(groups[::-1], axis=0)

    flags = jnp.broadcast_to(blow[...].astype(f32), (8, rows))
    a, b = iota((rows, 128), 0), iota((rows, 128), 1)
    mirror_out[total:total + 8] = place(flags, b == 2 * rows + rows - 1 - a)
    for copy in copies:
        copy.wait()
    for c in range(FIELDS):
        block = wall_strips(lambda k, c=c: pert[c, :, k, :], PLANES)
        mirror_out[c * rows:(c + 1) * rows] = reverse(block) * HELD
    mirror_out[own:total] = reverse(wall_strips(lambda q: coefs[q], 3))


def pack_strips_kernel(
    rows, me_ref, strips, even_in, odd_in, even_out, odd_out, stage, sems
):
    is_odd = me_ref[0] % 2
    own = rows * FIELDS
    b, a = iota((128, 128), 1), iota((128, 128), 0)
    copies = []
    for p, (out, first) in enumerate(((even_out, 1), (odd_out, 0))):
        parts = [
            head_or_tail(is_odd, strips[c * rows:(c + 1) * rows], first)
            for c in range(FIELDS)
        ]
        parts.append(jnp.zeros((6, 128), f32))
        parts.append(head_or_tail(is_odd, strips[own:own + rows], first))
        parts.append(jnp.zeros((24 - HALO, 128), f32))
        start = jnp.where(is_odd == first, 0, rows - HALO)
        base = own + 2 * HALO - 128
        parts.append(place(
            strips[own + rows:own + rows + 8],
            (b - base == a - 2 * rows - start) & (b >= base) & (b < base + HALO),
        ))
        block = jnp.concatenate(parts, axis=0)
        stage[p, :, 0:128] = block[0:64]
        stage[p, :, 128:256] = block[64:128]
        copy = pltpu.make_async_copy(
            stage.at[p], out.at[pl.ds(PAYLOAD, 64)], sems.at[p]
        )
        copy.start()
        copies.append(copy)
    for copy in copies:
        copy.wait()


def segments(block, hold, mid, store):
    hold[...] = block.T
    for js in range(SEGMENTS):
        for low in range(4):
            mid[low * 64 + js * 8:low * 64 + js * 8 + 8] = hold[
                pl.ds(js * 32 + low, 8, stride=4), :
            ]
    for low in range(4):
        for part in range(8):
            store(part * 4 + low, mid[pl.ds(low * 64 + part, SEGMENTS, stride=8), :])


def from_segments(load, hold, mid):
    for low in range(4):
        for part in range(8):
            mid[pl.ds(low * 64 + part, SEGMENTS, stride=8), :] = load(part * 4 + low)
    for js in range(SEGMENTS):
        for low in range(4):
            hold[pl.ds(js * 32 + low, 8, stride=4), :] = mid[
                low * 64 + js * 8:low * 64 + js * 8 + 8
            ]
    return hold[...].T


def prepare_kernel(
    rows, me_ref, cut_ref, cxi, ceta, cspan, pert_hbm, ax_hbm, ae_hbm, sp_hbm, blow,
    even_out, odd_out, xt, ct, last_field, wide, narrow, cuts,
    pert, coefs, hold, mid, sems,
):
    is_odd = me_ref[0] % 2
    copies = [pltpu.make_async_copy(pert_hbm, pert, sems.at[0])]
    for q, ref in enumerate((ax_hbm, ae_hbm, sp_hbm)):
        copies.append(pltpu.make_async_copy(ref, coefs.at[q], sems.at[1 + q]))
    for copy in copies:
        copy.start()
    own = rows * FIELDS
    cuts[...] = jnp.where(iota((8, 128), 0) == 0, cut_ref[0], cut_ref[1])
    slots = rows + HALO
    rc, rs, _ = lane_index((LANES, LANES), 0, rows)
    cc, cs, _ = lane_index((LANES, LANES), 1, rows)
    apart = jnp.where((rs >= 0) & (cs >= 0), (rs - cs + slots) % slots, 0)
    band = jnp.zeros((LANES, LANES), f32)
    for d, value in ((1, 45.0), (2, -9.0), (3, 1.0)):
        band = jnp.where(apart == d, value, band)
        band = jnp.where(apart == slots - d, -value, band)
    same = ((rs == cs) & (rs >= 0)).astype(f32)
    col_comp, _, _ = lane_index((1, LANES), 1, rows)

    def spread(matrix):
        total = jnp.zeros((LANES, LANES), f32)
        for d in range(FIELDS):
            line = jnp.zeros((1, LANES), f32)
            for c in range(FIELDS):
                line = jnp.where(col_comp == c, matrix[c, d], line)
            total = jnp.where(rc == d, line, total)
        return total

    xi = spread(cxi) * band * (-time_step / 60.0)
    eta = spread(ceta) * same * (-time_step * 45.0 / 60.0)
    span = spread(cspan) * same * (-time_step * 0.5)
    grad = jnp.where(rc == cc, band, 0.0)
    for w, first, small in ((xi, 0, 0), (eta, 2, 1), (grad, 4, 2), (span, 5, 3)):
        hi, lo = split(w)
        wide[first * LANES:(first + 1) * LANES] = hi
        if first != 4:
            wide[(first + 1) * LANES:(first + 2) * LANES] = lo
        narrow[small * LANES:(small + 1) * LANES] = w.astype(f8)
    for copy in copies:
        copy.wait()
    a, b = iota((rows, LANES), 0), iota((rows, LANES), 1)
    flags = jnp.broadcast_to(blow[...].astype(f32), (8, rows))
    for out, first in ((even_out, 1), (odd_out, 0)):
        for k in range(PLANES):
            for c in range(FIELDS):
                out[k * EDGE + c * HALO:k * EDGE + (c + 1) * HALO] = head_or_tail(
                    is_odd, pert[c, :, k, :], first
                ) * HELD
        for q in range(3):
            out[COEFS + q * HALO:COEFS + (q + 1) * HALO] = head_or_tail(is_odd, coefs[q], first)
        out[COEFS + 3 * HALO:FLAGS] = jnp.zeros((FLAGS - COEFS - 3 * HALO, LANES), f32)
        start = jnp.where(is_odd == first, 0, rows - HALO)
        base = own + 2 * HALO
        out[FLAGS:PAYLOAD] = place(flags, (b - base == a - start) & (b >= base) & (b < base + HALO))
        out[PAYLOAD:PAYLOAD + 64] = jnp.zeros((64, LANES), f32)
    for k in range(PLANES):
        block = HELD * jnp.concatenate([pert[c, :, k, :] for c in range(FIELDS - 1)], axis=0)

        def store(jl, slab, k=k):
            xt[k, jl] = slab

        segments(block, hold.at[k], mid.at[k], store)
        last_field[k] = pert[FIELDS - 1, :, k, :] * HELD
    for q in range(3):
        block = jnp.concatenate([coefs[q] * SCALES[q] + KEEPS[q]] * (FIELDS - 1), axis=0)

        def store(jl, slab, q=q):
            ct[q, jl] = slab

        segments(block, hold.at[PLANES + q], mid.at[PLANES + q], store)


def window_kernel(
    rows, total_rows, second, me_ref, blow, strips, xt, ct, last_field,
    wide, narrow, cuts, halo_in, *rest,
):
    if second:
        xe, ge, ce, gce, le = rest[:5]
        out, rest = rest[5], rest[6:]
    else:
        xe, ge, ce, gce, le = rest[:5]
        rest = rest[5:]
    (
        xs, v0, gs, gv, zz, partial, high, low, span_high, span_low,
        coef, gcoef, lanes_ref, wx, wx8, hold, mid, ghold,
    ) = rest
    me = me_ref[0]
    is_odd = me % 2
    own = rows * FIELDS
    slots = rows + HALO
    rs = lane_index((LANES, LANES), 0, rows)[1]

    def set_xi_weights(low, high):
        keep = jnp.where((rs >= low) & (rs < high), 0.0, 1.0)
        for source, kept, masked in ((wide, wx, (0, 1, 4)), (narrow, wx8, (0, 2))):
            for t in masked:
                block = source[t * LANES:(t + 1) * LANES]
                kept[t * LANES:(t + 1) * LANES] = (block.astype(f32) * keep).astype(block.dtype)

    def dot(a, w):
        return jnp.dot(a, w, preferred_element_type=f32)

    def twice(a):
        return jnp.concatenate([a, a], axis=1)

    def couple_ij(xh, eh, low):
        n = LANES
        first = dot(jnp.concatenate([xh, xh, eh, eh], axis=1), wx[0:4 * n])
        first8 = dot(low, wx8[0:2 * n])
        grad = dot(xh, wx[4 * n:5 * n])
        grad8 = dot(low[:, 0:n], wx8[2 * n:3 * n])
        return first, first8, grad, grad8

    def couple_k(sh, sl):
        n = LANES
        return dot(twice(sh), wx[5 * n:7 * n]) + dot(sl, wx8[3 * n:4 * n])

    comp, slot, is_own = lane_index((1, LANES), 1, rows)
    sign = jnp.where(comp == 2, -1.0, 1.0).astype(f32)
    a, b = iota((rows, LANES), 0), iota((rows, LANES), 1)
    own_flags = place(
        jnp.broadcast_to(blow[...].astype(f32), (8, rows)), b == 2 * rows + a
    )
    own_mirror = jnp.concatenate(
        [strips[own + rows:own + rows + 8], jnp.zeros((8, LANES - 128), f32)], axis=1
    )

    def cut_lanes(g):
        i = me * rows + g - HALO
        mirror = total_rows - 1 - i
        low, high = cuts[0:1, 0:1], cuts[1:2, 0:1]
        inside = ((i >= low) & (i < high)) | ((mirror >= low) & (mirror < high))
        return inside.astype(f32)

    def read_window(halo, halo_right):
        for k in range(PLANES):
            xs[k, 3:35, :, 0:128] = xt[k]
            v0[k, :, :, 0:128] = xt[k]

            def store(jl, slab, k=k):
                xs[k, 3 + jl, :, 128:256] = slab
                v0[k, jl, :, 128:256] = slab

            segments(
                jnp.concatenate(
                    [last_field[k], halo[k * EDGE:(k + 1) * EDGE], jnp.zeros((6, LANES), f32)],
                    axis=0,
                ),
                hold.at[k], mid.at[k], store,
            )
        for q in range(3):
            coef[q, :, :, 0:128] = ct[q]
            edge = halo[COEFS + q * HALO:COEFS + (q + 1) * HALO] * SCALES[q] + KEEPS[q]
            block = jnp.concatenate(
                [jnp.zeros((rows, LANES), f32)] + [edge] * FIELDS
                + [jnp.zeros((128 - rows - FIELDS * HALO, LANES), f32)], axis=0,
            )
            lane = iota((1, 128), 1)

            def store(jl, slab, q=q):
                coef[q, jl, :, 128:256] = jnp.where(lane < rows, ct[q, jl], slab)

            segments(block, hold.at[PLANES + q], mid.at[PLANES + q], store)
        near, far = halo[PAYLOAD:PAYLOAD + 64, 0:128], halo[PAYLOAD:PAYLOAD + 64, 128:256]
        last = strips[(FIELDS - 1) * rows:own]
        left = strips[0:128].T
        right = jnp.concatenate([last, near, far[0:32]], axis=0).T
        ghold[0, 0:128], ghold[0, 128:256] = left, right
        for m in range(HALO):
            for t in range(2):
                line = ghold[0, pl.ds(t * 128 + m, PLANES, stride=STRIP), :]
                gs[3 + m, 0:4, t * 128:(t + 1) * 128] = line
                gs[3 + m, 4:8, t * 128:(t + 1) * 128] = line
                gv[m, 0:4, t * 128:(t + 1) * 128] = line
                gv[m, 4:8, t * 128:(t + 1) * 128] = line
        mine, edge = strips[own:own + rows], far[32:32 + HALO]
        ghold[1, 0:128] = jnp.concatenate([mine] * (FIELDS - 1), axis=0).T
        ghold[1, 128:256] = jnp.concatenate(
            [mine] + [edge] * FIELDS
            + [jnp.zeros((128 - rows - FIELDS * HALO, 128), f32)], axis=0,
        ).T
        for q in range(3):
            for m in range(HALO):
                for t in range(2):
                    at = t * 128 + q * STRIP + m
                    gcoef[q, m, :, t * 128:(t + 1) * 128] = jnp.broadcast_to(
                        ghold[1, at:at + 1, :] * SCALES[q] + KEEPS[q], (8, 128)
                    )
        g = jnp.where(is_own, slot, jnp.where(halo_right == 1, slots + slot, slot))
        lanes_ref[0] = jnp.broadcast_to(cut_lanes(g), (8, LANES))
        lanes_ref[1] = 2.0 * (own_flags + halo[FLAGS:PAYLOAD])
        lanes_ref[2] = 2.0 * (
            own_mirror + jnp.concatenate([jnp.zeros((8, 128), f32), far[56:64]], axis=1)
        )

    sub = iota((8, LANES), 0)

    def pressure(line):
        near = pltpu.roll(line, LANES - 2 * rows, axis=1)
        far = pltpu.roll(line, LANES - 2 * HALO, axis=1)
        return jnp.where(is_own, near, far)

    def slopes(load, offset):
        return (
            (load(offset + 1) - load(offset - 1))
            - 0.2 * (load(offset + 2) - load(offset - 2))
            + (1.0 / 45.0) * (load(offset + 3) - load(offset - 3))
        )

    def time_stage(depth, alpha, beta):
        cut = lanes_ref[0] > 0.5
        wall = []
        for m in range(3):
            line = jnp.concatenate([xs[k, 3 + m, 0:1, :] for k in range(PLANES)], axis=0)
            wall.append(jnp.concatenate([line, line], axis=0))
        wall_g = [gs[3 + m] for m in range(3)]
        lift = lanes_ref[1] * jnp.where(comp == 2, pressure(wall[0]), 0.0)
        lift_g = lanes_ref[2] * jnp.where(comp == 2, pressure(wall_g[0]), 0.0)
        for m in range(3):
            ghost = jnp.where(cut, sign * wall_g[m], sign * wall[m] + lift)
            gs[2 - m] = jnp.where(cut, sign * wall[m], sign * wall_g[m] + lift_g)
            for k in range(PLANES):
                below = pltpu.roll(xs[k, 34 - m], 1, axis=0)
                xs[k, 2 - m] = jnp.where(sub == 0, ghost[k:k + 1], below)
                above = pltpu.roll(xs[k, 3 + m], SEGMENTS - 1, axis=0)
                xs[k, 35 + m] = jnp.where(sub == SEGMENTS - 1, 0.0, above)
        rows8 = 8 * SEGMENTS
        chunks = [(8 * c, slice(rows8 * c, rows8 * (c + 1))) for c in range(4)]

        def flat(v):
            return v.reshape(rows8, LANES)

        def split_plane(k):
            for at, here in chunks:
                x = flat(xs[k, 3 + at:11 + at])
                e = flat(slopes(lambda o: xs[k, at + o:at + o + 8], 3))
                cb, cd = flat(coef[1, at:at + 8]), flat(coef[2, at:at + 8])
                partial[k, here] = cb * e + cd * x
                xh, xl = split_small(x)
                eh, el = split_small(e)
                high[k, here, 0:LANES] = xh
                high[k, here, LANES:2 * LANES] = eh
                low[k, here, 0:LANES] = xl
                low[k, here, LANES:2 * LANES] = el

        for p in range(2):
            for at, here in chunks:
                s = xs[p + 1, 3 + at:11 + at] - xs[(p + 3) % PLANES, 3 + at:11 + at]
                span_high[p, here], span_low[p, here] = split_small(flat(s))
        split_plane(0)
        for p in range(2):
            zz[p] = couple_k(span_high[p], span_low[p])
        for k in range(PLANES):
            first, first8, grad, grad8 = couple_ij(
                high[k, :, 0:LANES], high[k, :, LANES:2 * LANES], low[k]
            )
            if k + 1 < PLANES:
                split_plane(k + 1)
            for at, here in chunks:
                ca = flat(coef[0, at:at + 8])
                r = (first[here] + first8[here]) + ca * (grad[here] + grad8[here])
                r = r + partial[k, here]
                r = r + zz[k, here] if k < 2 else r - zz[k - 2, here]
                if not isinstance(alpha, float) or alpha:
                    r = alpha * flat(v0[k, at:at + 8]) + beta * r
                xs[k, 3 + at:11 + at] = r.reshape(8, SEGMENTS, LANES)
        if not depth:
            return
        n = depth * 8
        x = gs[3:3 + depth].reshape(n, LANES)
        e = slopes(lambda at: gs[at:at + depth], 3).reshape(n, LANES)
        xh, xl = split_small(x)
        eh, el = split_small(-e)
        first, first8, grad, grad8 = couple_ij(xh, eh, jnp.concatenate([xl, el], axis=1))
        s = gs[3:3 + depth]
        s = pltpu.roll(s, 7, axis=1) - pltpu.roll(s, 1, axis=1)
        z = couple_k(*split_small(s.reshape(n, LANES)))
        ca, cb, cd = (gcoef[q, 0:depth].reshape(n, LANES) for q in range(3))
        r = cb * e + cd * x - (first + first8) - ca * (grad + grad8) + z
        r = r.reshape(depth, 8, LANES)
        if not isinstance(alpha, float) or alpha:
            r = alpha * gv[0:depth] + beta * r
        gs[3:3 + depth] = r

    def time_steps(depth):
        weights = ((0.0, 1.0), (0.75, 0.25), (1.0 / 3.0, 2.0 / 3.0))
        if second:
            for n, (alpha, beta) in enumerate(weights):
                time_stage(-(-(depth - 3 * n) // 4) * 4, alpha, beta)
            return

        def stage(s, carry):
            alpha, beta = (
                jnp.where(s == 0, w[0], jnp.where(s == 1, w[1], w[2])).astype(f32)
                for w in zip(*weights)
            )
            time_stage(depth, alpha, beta)
            return carry

        lax.fori_loop(0, 3, stage, 0)

    at_start = me == 0
    at_end = me == total_rows // rows - 1
    gs[...] = jnp.zeros(gs.shape, f32)
    if not second:
        wx[...] = wide[...]
        wx8[...] = narrow[...]
        read_window(halo_in, 1 - is_odd)
        time_steps(HALO - 2)
        for k in range(PLANES):
            xe[k] = xs[k, 3:35]
        ge[...] = gs[3:3 + REACH]
        for q in range(3):
            ce[q] = coef[q, :, :, 128:256]
        gce[...] = gcoef[:, 0:REACH]
        le[...] = lanes_ref[...]
        return
    outside = at_start | at_end
    wx[...] = wide[...]
    wx8[...] = narrow[...]

    @pl.when(outside)
    def _():
        set_xi_weights(0, HALO)

    read_window(halo_in, is_odd)
    time_steps(HALO - 3)
    @pl.when(outside)
    def _():
        set_xi_weights(jnp.where(at_start, REACH, 0), jnp.where(at_start, HALO, REACH))

    left = (slot >= REACH) & (slot < REACH + rows)
    from_e = jnp.where(left, is_odd, 1 - is_odd) == 1
    for k in range(PLANES):
        merged = jnp.where(from_e, xe[k], xs[k, 3:35])
        xs[k, 3:35] = merged
        v0[k] = merged
    merged = jnp.where(from_e, ge[...], gs[3:3 + REACH])
    gs[3:3 + REACH] = merged
    gv[0:REACH] = merged
    coef[:, :, :, 128:256] = jnp.where(from_e[:, 128:256], ce[...], coef[:, :, :, 128:256])
    gcoef[:, 0:REACH] = jnp.where(from_e, gce[...], gcoef[:, 0:REACH])
    g = jnp.where(is_own, slot, jnp.where(slot < REACH, slots + slot, slot))
    lanes_ref[0] = jnp.broadcast_to(cut_lanes(g), (8, LANES))
    lanes_ref[1] = jnp.where(from_e, le[1], lanes_ref[1])
    lanes_ref[2] = jnp.where(from_e, le[2], lanes_ref[2])
    time_steps(REACH - 3)
    for k in range(PLANES):
        block = from_segments(
            lambda jl: xs[k, 3 + jl, :, 0:128], hold.at[k], mid.at[k]
        ) * (1.0 / HELD)
        for c in range(FIELDS - 1):
            out[c, :, k, :] = block[c * rows:(c + 1) * rows]
    lane = iota((1, 128), 1)

    def last_lanes(jl):
        line = xs[0, 3 + jl, :, 128:256]
        for k in range(1, PLANES):
            moved = pltpu.roll(xs[k, 3 + jl, :, 128:256], k * rows, axis=1)
            line = jnp.where(lane >= k * rows, moved, line)
        return line

    block = from_segments(last_lanes, hold.at[PLANES], mid.at[PLANES]) * (1.0 / HELD)
    for k in range(PLANES):
        out[FIELDS - 1, :, k, :] = block[k * rows:(k + 1) * rows]


def on_device(
    perturbation, advect_xi, advect_eta, sponge,
    couple_xi, couple_eta, couple_span, wake_cut, blowing,
):
    rows = perturbation.shape[1]
    devices = lax.axis_size("wrap")
    total_rows = rows * devices
    own = rows * FIELDS
    me = lax.axis_index("wrap").astype(jnp.int32).reshape(1)
    flags = blowing.reshape(1, rows)
    mirror = [(i, devices - 1 - i) for i in range(devices)]
    same_chip = [(i, i ^ 1) for i in range(devices)]
    next_chip = [(i, i + 1 if i % 2 else i - 1) for i in range(1, devices - 1)]

    vmem = pl.BlockSpec(memory_space=pltpu.VMEM)
    smem = pl.BlockSpec(memory_space=pltpu.SMEM)
    hbm = pl.BlockSpec(memory_space=pltpu.HBM)
    anywhere = pl.BlockSpec(memory_space=pl.ANY)

    def call(kernel, outs, ins, scratch, us, out_specs=None, vmem_kib=32 * 1024, **more):
        return pl.pallas_call(
            kernel,
            out_shape=outs,
            in_specs=ins,
            out_specs=out_specs or (vmem,) * len(outs),
            scratch_shapes=scratch,
            compiler_params=pltpu.CompilerParams(vmem_limit_bytes=vmem_kib * 1024),
            cost_estimate=pl.CostEstimate(
                flops=int(us * 1e9), bytes_accessed=int(us * 3e6), transcendentals=0
            ),
            **more,
        )

    def shape(*dims, dtype=f32):
        return jax.ShapeDtypeStruct(dims, dtype)

    dma = pltpu.SemaphoreType.DMA
    (to_mirror,) = call(
        functools.partial(pack_mirror_kernel, rows),
        (shape(own + rows + 8, 128),),
        [hbm] * 4 + [vmem],
        [
            pltpu.VMEM((FIELDS, rows, PLANES, 128), f32),
            pltpu.VMEM((3, rows, 128), f32),
            dma((FIELDS + 3,)),
        ],
        1,
        vmem_kib=64600,
    )(perturbation, advect_xi, advect_eta, sponge, flags)
    strips = lax.ppermute(to_mirror, "wrap", mirror)

    state = (PLANES, 32, SEGMENTS, LANES)
    payload = shape(PAYLOAD + 64, LANES)
    even, odd, xt, ct, last_field, wide, narrow, cuts = call(
        functools.partial(prepare_kernel, rows),
        (
            payload, payload,
            shape(PLANES, 32, SEGMENTS, 128), shape(3, 32, SEGMENTS, 128),
            shape(PLANES, rows, LANES),
            shape(7 * LANES, LANES, dtype=bf16), shape(4 * LANES, LANES, dtype=f8),
            shape(8, 128, dtype=jnp.int32),
        ),
        [smem] * 5 + [hbm] * 4 + [vmem],
        [
            pltpu.VMEM((FIELDS, rows, PLANES, LANES), f32),
            pltpu.VMEM((3, rows, LANES), f32),
            pltpu.VMEM((PLANES + 3, LANES, 128), f32),
            pltpu.VMEM((PLANES + 3, LANES, 128), f32),
            dma((4,)),
        ],
        4,
    )(
        me, wake_cut, couple_xi, couple_eta, couple_span,
        perturbation, advect_xi, advect_eta, sponge, flags,
    )
    even, odd = call(
        functools.partial(pack_strips_kernel, rows),
        (payload, payload),
        [smem, vmem, anywhere, anywhere],
        [pltpu.VMEM((2, 64, LANES), f32), dma((2,))],
        1,
        out_specs=(anywhere, anywhere),
        input_output_aliases={2: 0, 3: 1},
    )(me, strips, even, odd)
    from_next = lax.ppermute(odd, "wrap", next_chip)
    from_same = lax.ppermute(even, "wrap", same_chip)

    scratch = [
        pltpu.VMEM((PLANES, 38, SEGMENTS, LANES), f32),
        pltpu.VMEM(state, f32),
        pltpu.VMEM((3 + HALO + 3, 8, LANES), f32),
        pltpu.VMEM((HALO, 8, LANES), f32),
        pltpu.VMEM((2, LANES, LANES), f32),
        pltpu.VMEM((PLANES, LANES, LANES), f32),
        pltpu.VMEM((PLANES, LANES, 2 * LANES), bf16),
        pltpu.VMEM((PLANES, LANES, 2 * LANES), f8),
        pltpu.VMEM((2, LANES, LANES), bf16),
        pltpu.VMEM((2, LANES, LANES), f8),
        pltpu.VMEM((3, 32, SEGMENTS, LANES), f32),
        pltpu.VMEM((3, HALO, 8, LANES), f32),
        pltpu.VMEM((3, 8, LANES), f32),
        pltpu.VMEM((7 * LANES, LANES), bf16),
        pltpu.VMEM((4 * LANES, LANES), f8),
        pltpu.VMEM((PLANES + 3, LANES, 128), f32),
        pltpu.VMEM((PLANES + 3, LANES, 128), f32),
        pltpu.VMEM((2, LANES, 128), f32),
    ]
    common = (me, flags, strips, xt, ct, last_field, wide, narrow, cuts)
    specs = [smem] + [vmem] * 8
    first = call(
        functools.partial(window_kernel, rows, total_rows, False),
        (
            shape(*state), shape(REACH, 8, LANES), shape(3, 32, SEGMENTS, 128),
            shape(3, REACH, 8, LANES), shape(3, 8, LANES),
        ),
        specs + [vmem], scratch, 8,
    )(*common, from_same)
    (out,) = call(
        functools.partial(window_kernel, rows, total_rows, True),
        (shape(*perturbation.shape),),
        specs + [vmem] * 6, scratch, 14,
    )(*common, from_next, *first)
    return out


def solution(mesh):
    in_specs = (
        P(None, "wrap", None, None),
        P("wrap", None),
        P("wrap", None),
        P("wrap", None),
        P(),
        P(),
        P(),
        P(),
        P("wrap"),
    )
    out_specs = P(None, "wrap", None, None)
    return jax.shard_map(
        on_device, mesh=mesh, in_specs=in_specs, out_specs=out_specs, check_vma=False
    )
```
